128 devices in a mesh: tile: 64 (over y, z, x), chan: 2 (over core).
Axes of the slice: x: 4, y: 4, z: 4, core: 2. Of those that a mesh axis runs over, the one named last changes fastest.
Arguments:
- attributes: bfloat16 [35, 1024, 512], P(None, 'tile'), may hold values from -6 to 6
- cell_basin: int32 [1024, 512], P('tile'), may hold values from 0 to 8191, as said below
- basin_cells: int32 [8192], P('tile'), may hold values from 1 to 127, as said below
- conv_first: bfloat16 [128, 3, 3, 35], P('chan'), may hold values from -0.5 to 0.5
- conv_second: bfloat16 [128, 3, 3, 128], P('chan'), may hold values from -0.25 to 0.25
- conv_third: bfloat16 [128, 3, 3, 128], P('chan'), may hold values from -0.25 to 0.25
- head_weight: bfloat16 [128, 12], P('chan'), may hold values from -0.75 to 0.75
- precip: float32 [30, 16, 8192], P(None, 'chan', 'tile'), may hold values from 0 to 250
- temp: float32 [30, 16, 8192], P(None, 'chan', 'tile'), may hold values from -24 to 24
- pet: float32 [30, 16, 8192], P(None, 'chan', 'tile'), may hold values from 0.5 to 4
Outputs:
- streamflow: float32 [30, 16, 8192], P(None, 'chan', 'tile')
The draws below stay inside these ranges and needn't reach their ends.
Inputs may be any that keep to these rules, and one draw needn't show every extreme that they name: `cell_basin`: in each tile the 8192 cells in row-major order form 64 runs of 128 cells; the runs of one tile go to 64 different owners, so that every owner receives exactly 128 cells from every tile. The basins of owner o are o * 128 to o * 128 + 127; one run holds 2 whole basins, each a contiguous part of the run. `basin_cells`: the number of cells of cell_basin in each basin; some basin reaches the most.
All inputs are finite; a program needn't handle non-finite values.
Results may differ from the reference program's by a relative error of at most 0.00061.
Values may be sent and summed in bfloat16 or wider, within the bound.
A program may use at most 64 MiB of HBM per device.

```python
import jax
import jax.numpy as jnp
from jax import lax

A = 35
C = 128
P_SIZE = 12
LAGS = 15
TH = 16
W = 512
B_DEV = 128
DAYS = 30
WIN = 16
NROWS = 1024
NB = 8192
CAP = 128
BPG = 2
N_TILE = 64


def basin_layout(key):
    offsets = jax.random.permutation(jax.random.fold_in(key, 11), N_TILE).astype(jnp.int32)
    source = jnp.arange(N_TILE, dtype=jnp.int32)[:, None]
    owner = (source + offsets[None, :]) % N_TILE
    weights = jax.random.randint(jax.random.fold_in(key, 12), (N_TILE, N_TILE, BPG), 1, 5)
    weights = weights * weights
    keep_first = (jnp.arange(BPG, dtype=jnp.int32) == 0).astype(jnp.int32)
    weights = weights.at[0, 0].set(weights[0, 0] * keep_first)
    running = jnp.cumsum(weights, axis=2)
    ends = jnp.arange(1, BPG + 1, dtype=jnp.int32)[None, None, :] + (CAP - BPG) * running // running[:, :, -1:]
    position = jnp.arange(CAP, dtype=jnp.int32)
    inner = jnp.sum((position[None, None, :, None] >= ends[:, :, None, :]).astype(jnp.int32), axis=3)
    group = jnp.arange(N_TILE, dtype=jnp.int32)[None, :, None]
    basin = owner[:, :, None] * B_DEV + group * BPG + inner
    return basin.reshape(NROWS, W).astype(jnp.int32)


def draw_cell_basin(key, part):
    return basin_layout(key)


def draw_basin_cells(key, part):
    ident = basin_layout(key).reshape(-1)
    return jax.ops.segment_sum(jnp.ones_like(ident), ident, num_segments=NB).astype(jnp.int32)


def draw_attributes(key, part):
    first_key = jax.random.fold_in(key, 21)
    second_key = jax.random.fold_in(key, 22)
    rough = jax.random.normal(first_key, (A, NROWS, W), jnp.float32)
    regional = jax.random.normal(second_key, (A, NROWS, W // 64, 1), jnp.float32)
    regional = jnp.broadcast_to(regional, (A, NROWS, W // 64, 64)).reshape(A, NROWS, W)
    field = jnp.clip(0.8 * rough + regional, -6.0, 6.0)
    return field.astype(jnp.bfloat16)


def draw_precip(key, part):
    base_key = jax.random.fold_in(key, 31)
    storm_key = jax.random.fold_in(key, 32)
    size_key = jax.random.fold_in(key, 33)
    shape = (DAYS, WIN, NB)
    background = jax.random.uniform(base_key, shape, jnp.float32, 0.0, 10.0)
    storms = jax.random.uniform(size_key, shape, jnp.float32, 60.0, 240.0)
    chance = 1.0 / 12.0
    struck = jax.random.uniform(storm_key, shape, jnp.float32, 0.0, 1.0) < chance
    return jnp.where(struck, storms, background).astype(jnp.float32)


def level_of(stream_key, dims, pieces, least, high):
    factor_of = 1.0
    for axis_at, shards_of in pieces:
        steps = jax.random.uniform(jax.random.fold_in(jax.random.fold_in(stream_key, 6), axis_at), (shards_of,), jnp.float32, least / len(pieces), high / len(pieces))
        factor_of = factor_of * jnp.repeat(jnp.exp(steps), dims[axis_at] // shards_of).reshape((-1,) + (1,) * (len(dims) - 1 - axis_at))
    return factor_of


def normal_values(rng, shape, width, limit, cuts=(), held_as=jnp.bfloat16):
    loudness = level_of(rng, shape, cuts, -0.22, 0.18) if cuts else 1.0
    values = jax.random.normal(rng, shape, jnp.float32) * width * loudness
    return jnp.minimum(jnp.maximum(values, -limit), limit).astype(held_as)


def setup_inputs(seed: int = 0) -> dict:
    arg_keys = jax.random.split(jax.random.key(seed), 11)
    attributes = draw_attributes(jax.random.fold_in(arg_keys[10], 71), 0)
    cell_basin = draw_cell_basin(jax.random.fold_in(arg_keys[10], 71), 0)
    basin_cells = draw_basin_cells(jax.random.fold_in(arg_keys[10], 71), 0)
    conv_first = normal_values(arg_keys[3], (C, 3, 3, A), (9 * A // 2) ** -0.5, 0.5, ((0, 2),))
    conv_second = normal_values(arg_keys[4], (C, 3, 3, C), (9 * C // 2) ** -0.5, 0.25, ((0, 2),))
    conv_third = normal_values(arg_keys[5], (C, 3, 3, C), (9 * C // 2) ** -0.5, 0.25, ((0, 2),))
    head_weight = normal_values(arg_keys[6], (C, P_SIZE), (C // 2) ** -0.5, 0.75, ((0, 2),))
    precip = draw_precip(jax.random.fold_in(arg_keys[10], 71), 0)
    temp = normal_values(arg_keys[8], (DAYS, WIN, NB), 6.0, 24.0, ((1, 2), (2, 64)), jnp.float32)
    pet = jnp.clip(0.5 + 3.5 * jax.random.uniform(arg_keys[9], (DAYS, WIN, NB), jnp.float32) ** level_of(arg_keys[9], (DAYS, WIN, NB), ((1, 2), (2, 64)), -0.2, 0.2), 0.5, 4.0)
    return dict(attributes=attributes, cell_basin=cell_basin, basin_cells=basin_cells, conv_first=conv_first, conv_second=conv_second, conv_third=conv_third, head_weight=head_weight, precip=precip, temp=temp, pet=pet)


LOW = [-2.0, 0.5, 50.0, 1.0, 0.3, 0.05, 0.01, 0.001, 0.0, 0.5, 1.0, 0.5]
SPAN = [4.0, 5.5, 450.0, 4.0, 0.7, 0.45, 0.29, 0.099, 50.0, 5.5, 2.0, 2.5]


def conv_band(field, weight):
    kernel = jnp.transpose(weight.astype(jnp.float32), (0, 3, 1, 2))
    out = lax.conv_general_dilated(field[None], kernel, (1, 1), ((0, 0), (1, 1)),
                                   dimension_numbers=("NCHW", "OIHW", "NCHW"),
                                   precision=lax.Precision.HIGHEST)
    return out[0]


def bucket_run(param, precip, temp, pet):
    tt, cfmax, fc, beta, lp = param[0], param[1], param[2], param[3], param[4]
    k0, k1, k2, uzl, perc = param[5], param[6], param[7], param[8], param[9]

    def day(state, force):
        snow, soil, upper, lower = state
        rain_in, air, demand = force
        liquid = jax.nn.sigmoid(air - tt)
        gained = snow + rain_in * (1.0 - liquid)
        snow_new = jnp.maximum(gained - cfmax * jnp.maximum(air - tt, 0.0), 0.0)
        melt = gained - snow_new
        inflow = rain_in * liquid + melt
        recharge = inflow * jnp.power(soil / fc, beta)
        soil = soil + inflow - recharge
        excess = jnp.maximum(soil - fc, 0.0)
        soil = soil - excess
        soil = jnp.where(soil < lp * fc, soil * (1.0 - demand / (lp * fc)), soil - demand)
        upper = upper + recharge + excess
        upper_new = jnp.maximum(upper - perc, 0.0)
        lower = lower + upper - upper_new
        quick = k0 * jnp.maximum(upper_new - uzl, 0.0)
        slow = k1 * upper_new
        upper = upper_new - quick - slow
        base = k2 * lower
        lower = lower - base
        return (snow_new, soil, upper, lower), quick + slow + base

    shape = precip.shape[1:]
    start = (jnp.zeros(shape, jnp.float32), jnp.broadcast_to(0.5 * fc, shape),
             jnp.full(shape, 5.0, jnp.float32), jnp.full(shape, 20.0, jnp.float32))
    final, runoff = lax.scan(day, start, (precip, temp, pet))
    return runoff


def route(param, runoff):
    days = runoff.shape[0]
    lag = jnp.arange(LAGS).astype(jnp.float32) + 0.5
    weight = jnp.exp((param[10] - 1.0)[None, :] * jnp.log(lag)[:, None] - lag[:, None] / param[11][None, :])
    weight = weight / jnp.sum(weight, axis=0, keepdims=True)
    later = jnp.arange(days)[:, None] - jnp.arange(days)[None, :]
    pick = (later[None, :, :] == jnp.arange(LAGS)[:, None, None]).astype(jnp.float32)
    matrix = jnp.einsum("kts,kb->tsb", pick, weight, precision=lax.Precision.HIGHEST)
    return jnp.einsum("tsb,swb->twb", matrix, runoff, precision=lax.Precision.HIGHEST)


def reference(attributes, cell_basin, basin_cells, conv_first, conv_second, conv_third, head_weight, precip, temp, pet):
    padded = jnp.pad(attributes, ((0, 0), (3, 3), (0, 0)))

    def one_band(band):
        first_row = band * TH
        field = lax.dynamic_slice_in_dim(padded, first_row, TH + 6, 1).astype(jnp.float32)
        layers = (conv_first, conv_second, conv_third)
        for depth in range(3):
            field = jnp.maximum(conv_band(field, layers[depth]), 0.0)
            count = TH + 4 - 2 * depth
            rows = first_row - 2 + depth + jnp.arange(count)
            inside = (rows >= 0) & (rows < NROWS)
            field = jnp.where(inside[None, :, None], field, 0.0)
            field = lax.optimization_barrier(field.astype(jnp.bfloat16)).astype(jnp.float32)
        raw = jnp.einsum("cp,chw->phw", head_weight.astype(jnp.float32), field, precision=lax.Precision.HIGHEST)
        return jax.nn.sigmoid(raw)

    shares = lax.map(one_band, jnp.arange(N_TILE))
    shares = jnp.transpose(shares, (1, 0, 2, 3)).reshape(P_SIZE, NROWS * W)
    sums = jax.ops.segment_sum(shares.T, cell_basin.reshape(-1), num_segments=NB)
    mean = sums.T / basin_cells.astype(jnp.float32)[None, :]
    param = jnp.array(LOW, jnp.float32)[:, None] + jnp.array(SPAN, jnp.float32)[:, None] * mean
    runoff = bucket_run(param, precip, temp, pet)
    return route(param, runoff)
```

```python
import jax
import jax.numpy as jnp
from jax import lax
from jax.experimental import pallas as pl
from jax.experimental.pallas import tpu as pltpu
from jax.sharding import PartitionSpec as P

LAGS = 15
LOW = [-2.0, 0.5, 50.0, 1.0, 0.3, 0.05, 0.01, 0.001, 0.0, 0.5, 1.0, 0.5]
SPAN = [4.0, 5.5, 450.0, 4.0, 0.7, 0.45, 0.29, 0.099, 50.0, 5.5, 2.0, 2.5]
MESH = pl.DeviceIdType.MESH
F32 = jnp.float32
BF16 = jnp.bfloat16

A = 35
TH = 16
HALF = 8
W = 512
NT = 64
CP = 64
SUB = 16
STEP = W // SUB
WP = W + 2 * SUB
HW0 = 576
TAPS2 = 592
TAPS3 = TAPS2 + 1152
WROWS = TAPS3 + 1152


def dot(a, b):
    return jnp.dot(a, b, preferred_element_type=F32)


def dot_nt(a, b):
    return lax.dot_general(a, b, (((1,), (1,)), ((), ())), preferred_element_type=F32)


def dot_tn(a, b):
    return lax.dot_general(a, b, (((0,), (0,)), ((), ())), preferred_element_type=F32)


def put_row(dst, row, a):
    sub = lax.broadcasted_iota(jnp.int32, (SUB, a.shape[1]), 0)
    dst[row, SUB : SUB + W, :] = a.astype(BF16)
    before = jnp.where(sub == 0, 0.0, pltpu.roll(a[W - SUB :], 1, axis=0))
    after = jnp.where(sub == SUB - 1, 0.0, pltpu.roll(a[:SUB], SUB - 1, axis=0))
    dst[row, :SUB, :] = before.astype(BF16)
    dst[row, SUB + W :, :] = after.astype(BF16)


def raster_kernel(
    attr, cb, w1, w2, w3, hw, out,
    spread, slots, perm, wsend, wrecv, wide1, wide2, wide3, wideh,
    h0, h1, h2, h3, maskb, sendb, recvb, sibb,
    halo_send, halo_recv, w_send, w_recv, row_send, row_recv, sib_send, sib_recv,
):
    tile = lax.axis_index("tile")
    chan = lax.axis_index("chan")
    barrier = pltpu.get_barrier_semaphore()

    def greet(i, carry):
        pl.semaphore_signal(
            barrier, inc=1, device_id={"tile": lax.rem(tile + i, NT)}, device_id_type=MESH
        )
        return carry

    lax.fori_loop(1, NT, greet, 0)
    pl.semaphore_signal(barrier, inc=1, device_id={"chan": 1 - chan}, device_id_type=MESH)

    flat = attr[...].reshape(A * TH, W)
    for g in range(4):
        spread[g, : A * TH, :] = flat[:, g * 128 : (g + 1) * 128].astype(F32)
        spread[g, A * TH :, :] = jnp.zeros((48 * TH - A * TH, 128), F32)
    for r in range(TH):
        for g in range(4):
            part = spread[g, pl.ds(r, 48, stride=TH), :]
            slots[(3 + r) * CP : (3 + r) * CP + 48, g * 128 : (g + 1) * 128] = part.astype(BF16)
        slots[(3 + r) * CP + 48 : (4 + r) * CP, :] = jnp.zeros((CP - 48, W), BF16)

    lane = lax.broadcasted_iota(jnp.int32, (128, 128), 1)
    mine = lane // 64 == chan
    wsend[:TAPS2, :] = jnp.zeros((TAPS2, 128), BF16)
    for t in range(9):
        w = w1[t // 3, t % 3].astype(F32)
        w = jnp.where(mine[:A], jnp.concatenate([w, w], axis=1), 0.0)
        wsend[t * CP : t * CP + A, :] = w.astype(BF16)
    w = hw[...].astype(F32)
    w = jnp.where(mine[:12], jnp.concatenate([w, w], axis=1), 0.0)
    wsend[HW0 : HW0 + 12, :] = w.astype(BF16)
    for base, ref in ((TAPS2, w2), (TAPS3, w3)):
        for t in range(9):
            w = ref[t // 3, t % 3].astype(F32)
            w = jnp.concatenate([w, w], axis=0).T
            wsend[base + t * 128 : base + (t + 1) * 128, :] = jnp.where(mine, w, 0.0).astype(BF16)

    pl.semaphore_wait(barrier, NT)
    other = lax.rem(tile + jnp.where(chan == 0, 1, NT - 1), NT)
    src_at = pl.multiple_of((16 - 13 * chan) * CP, CP)
    dst_at = pl.multiple_of(19 * chan * CP, CP)
    halo = pltpu.make_async_remote_copy(
        src_ref=slots.at[pl.ds(src_at, 3 * CP)],
        dst_ref=slots.at[pl.ds(dst_at, 3 * CP)],
        send_sem=halo_send,
        recv_sem=halo_recv,
        device_id={"tile": other},
        device_id_type=MESH,
    )
    halo.start()
    weights = []
    for k, (first, last) in enumerate(((0, TAPS2), (TAPS2, TAPS3), (TAPS3, WROWS))):
        weights.append(
            pltpu.make_async_remote_copy(
                src_ref=wsend.at[pl.ds(first, last - first)],
                dst_ref=wrecv.at[pl.ds(first, last - first)],
                send_sem=w_send.at[k],
                recv_sem=w_recv.at[k],
                device_id={"chan": 1 - chan},
                device_id_type=MESH,
            )
        )
        weights[-1].start()

    place = lax.broadcasted_iota(jnp.int32, (W, W), 0)
    column = lax.broadcasted_iota(jnp.int32, (W, W), 1)
    perm[...] = ((place % SUB) * STEP + place // SUB == column).astype(F32).astype(BF16)

    def arrange(block):
        at = pl.multiple_of((chan * HALF + 2 * block) * CP, 2 * CP)
        put_row(h0, block, dot_nt(perm[...], slots[pl.ds(at, 2 * CP), :]))

    def arrange_own(i, carry):
        arrange(i + 2 * (1 - chan))
        return carry

    def arrange_halo(i, carry):
        arrange(i + 5 * chan)
        return carry

    lax.fori_loop(0, 5, arrange_own, 0)

    own = cb[pl.ds(pl.multiple_of(chan * HALF, HALF), HALF), :]
    firsts, ids1, ids2, owners = [], [], [], []
    for g in range(4):
        run = own[:, g * 128 : (g + 1) * 128]
        first = run[:, :1]
        last = run[:, 127:]
        firsts.append((run == first).astype(F32))
        owners.append(first // 128)
        ids1.append((first % 128).astype(F32))
        ids2.append((last % 128).astype(F32))
    first_mask = jnp.concatenate(firsts, axis=1)
    spreadm = jnp.broadcast_to(first_mask[:, None, :], (HALF, 16, W)).reshape(HALF * 16, W)
    maskb[...] = dot_nt(perm[...], spreadm.astype(BF16))

    wide1[...] = jnp.zeros(wide1.shape, BF16)
    wide2[...] = jnp.zeros(wide2.shape, BF16)
    wide3[...] = jnp.zeros(wide3.shape, BF16)
    weights[0].wait_recv()
    for t in range(9):
        dy, dx = t // 3, t % 3
        w = wsend[t * CP : (t + 1) * CP, :] + wrecv[t * CP : (t + 1) * CP, :]
        for e in range(2):
            row = dy + e
            at = ((row // 2) * 3 + dx) * 128 + (row % 2) * CP
            wide1[at : at + CP, e * 128 : (e + 1) * 128] = w
    w = (wsend[HW0:TAPS2, :] + wrecv[HW0:TAPS2, :]).astype(F32)
    w = jnp.broadcast_to(w[None], (HALF, 16, 128)).reshape(128, 128).T
    for r in range(HALF):
        wideh[r * 128 : (r + 1) * 128, :] = jnp.where(lane // 16 == r, w, 0.0).astype(BF16)

    halo.wait_recv()
    top = jnp.logical_and(chan == 0, tile == 0)
    bottom = jnp.logical_and(chan == 1, tile == NT - 1)

    @pl.when(jnp.logical_or(top, bottom))
    def _():
        slots[pl.ds(dst_at, 3 * CP), :] = jnp.zeros((3 * CP, W), BF16)

    lax.fori_loop(0, 2, arrange_halo, 0)

    def first_conv(pair, carry):
        lhs = jnp.concatenate(
            [h0[pair + b, dx * SUB : dx * SUB + W, :] for b in range(2) for dx in range(3)], axis=1
        )
        acc = jnp.maximum(dot(lhs, wide1[...]), 0.0)
        put_row(h1, 2 * pair, acc[:, :128])
        put_row(h1, 2 * pair + 1, acc[:, 128:])
        return carry

    lax.fori_loop(0, 6, first_conv, 0)

    @pl.when(top)
    def _():
        h1[0:2] = jnp.zeros((2, WP, 128), BF16)

    @pl.when(bottom)
    def _():
        h1[10:12] = jnp.zeros((2, WP, 128), BF16)

    def widen(k, base, wide):
        weights[k].wait_recv()
        for t in range(9):
            dy, dx = t // 3, t % 3
            span = slice(base + t * 128, base + (t + 1) * 128)
            w = wsend[span, :] + wrecv[span, :]
            for e in range(2):
                at = ((dy + e) * 3 + dx) * 128
                wide[at : at + 128, e * 128 : (e + 1) * 128] = w

    def taps(src, pair):
        return jnp.concatenate(
            [
                src[2 * pair + dy, dx * SUB : dx * SUB + W, :]
                for dy in range(4)
                for dx in range(3)
            ],
            axis=1,
        )

    widen(1, TAPS2, wide2)

    def second_conv(pair, carry):
        acc = jnp.maximum(dot(taps(h1, pair), wide2[...]), 0.0)
        put_row(h2, 2 * pair, acc[:, :128])
        put_row(h2, 2 * pair + 1, acc[:, 128:])
        return carry

    lax.fori_loop(0, 5, second_conv, 0)

    @pl.when(top)
    def _():
        h2[0:1] = jnp.zeros((1, WP, 128), BF16)

    @pl.when(bottom)
    def _():
        h2[9:10] = jnp.zeros((1, WP, 128), BF16)

    widen(2, TAPS3, wide3)

    def third_conv(pair, carry):
        acc = jnp.maximum(dot(taps(h2, pair), wide3[...]), 0.0)
        h3[pair] = acc.astype(BF16)
        return carry

    lax.fori_loop(0, 4, third_conv, 0)

    raw = dot(jnp.concatenate([h3[q] for q in range(4)], axis=1), wideh[...])
    share = jax.nn.sigmoid(raw)
    m = maskb[...]
    part1 = share * m
    part2 = share * (1.0 - m)
    sub32 = lax.broadcasted_iota(jnp.int32, (HALF, 128), 0)
    lane32 = lax.broadcasted_iota(jnp.int32, (HALF, 128), 1)
    rows = []
    for g in range(4):
        pair = []
        for part, ids in ((part1, ids1), (part2, ids2)):
            s = jnp.sum(part.reshape(W // SUB, SUB, 128), axis=0)
            s = jnp.sum(s[4 * g : 4 * g + 4], axis=0, keepdims=True)
            v = jnp.where(lane32 // 16 == sub32, jnp.broadcast_to(s, (HALF, 128)), 0.0)
            for shift in (64, 32, 16):
                v = v + pltpu.roll(v, shift, axis=1)
            pair.append(jnp.where(lane32 % 16 == 12, jnp.broadcast_to(ids[g], (HALF, 128)), v))
        rows.append(jnp.where((lane32 // 16) % 2 == 0, pair[0], pair[1]))
    value = jnp.concatenate(rows, axis=0)
    hi = value.astype(BF16).astype(F32)
    mid = (value - hi).astype(BF16).astype(F32)
    low = value - hi - mid
    kind = lax.broadcasted_iota(jnp.int32, (32, 128), 1) // 32
    parts = jnp.where(kind == 0, hi, jnp.where(kind == 1, mid, jnp.where(kind == 2, low, 0.0)))
    lane128 = lax.broadcasted_iota(jnp.int32, (HALF, 128), 1)
    to_owner = jnp.concatenate(
        [(jnp.broadcast_to(o, (HALF, 128)) == lane128).astype(F32) for o in owners], axis=0
    )
    routed = dot_tn(to_owner.astype(BF16), parts.astype(BF16))[:NT]
    sendb[...] = routed.reshape(NT, 1, 128)
    recvb[tile] = sendb[tile]

    def row_copy(o):
        return pltpu.make_async_remote_copy(
            src_ref=sendb.at[o],
            dst_ref=recvb.at[tile],
            send_sem=row_send,
            recv_sem=row_recv,
            device_id={"tile": o},
            device_id_type=MESH,
        )

    def send_row(i, carry):
        row_copy(lax.rem(tile + i, NT)).start()
        return carry

    lax.fori_loop(1, NT, send_row, 0)
    rest = pl.ds(0, NT - 1)
    pltpu.make_async_copy(recvb.at[rest], recvb.at[rest], row_recv).wait()
    sib = pltpu.make_async_remote_copy(
        src_ref=recvb,
        dst_ref=sibb,
        send_sem=sib_send,
        recv_sem=sib_recv,
        device_id={"chan": 1 - chan},
        device_id_type=MESH,
    )
    sib.start()
    sib.wait_recv()
    got = recvb[...].reshape(NT, 128) + sibb[...].reshape(NT, 128)
    basin = lax.broadcasted_iota(jnp.int32, (NT, 128), 1).astype(F32)
    gotb = got.astype(BF16)
    sums = jnp.zeros((16, 128), F32)
    for b in range(2):
        hit = (jnp.broadcast_to(got[:, 16 * b + 12 : 16 * b + 13], (NT, 128)) == basin).astype(F32)
        placed = dot_tn(gotb, hit.astype(BF16))
        for k in range(3):
            sums = sums + placed[32 * k + 16 * b : 32 * k + 16 * b + 16]
    out[...] = sums

    pltpu.make_async_copy(sendb.at[rest], sendb.at[rest], row_send).wait()
    sib.wait_send()
    halo.wait_send()
    for copy in weights:
        copy.wait_send()


def raster(attributes, cell_basin, w1, w2, w3, hw):
    vmem = pl.BlockSpec(memory_space=pltpu.VMEM)
    return pl.pallas_call(
        raster_kernel,
        out_shape=jax.ShapeDtypeStruct((16, 128), F32),
        in_specs=[vmem] * 6,
        out_specs=vmem,
        scratch_shapes=[
            pltpu.VMEM((4, 48 * TH, 128), F32),
            pltpu.VMEM((22 * CP, W), BF16),
            pltpu.VMEM((W, W), BF16),
            pltpu.VMEM((WROWS, 128), BF16),
            pltpu.VMEM((WROWS, 128), BF16),
            pltpu.VMEM((768, 256), BF16),
            pltpu.VMEM((1536, 256), BF16),
            pltpu.VMEM((1536, 256), BF16),
            pltpu.VMEM((1024, 128), BF16),
            pltpu.VMEM((7, WP, 128), BF16),
            pltpu.VMEM((12, WP, 128), BF16),
            pltpu.VMEM((10, WP, 128), BF16),
            pltpu.VMEM((4, W, 256), BF16),
            pltpu.VMEM((W, 128), F32),
            pltpu.VMEM((NT, 1, 128), F32),
            pltpu.VMEM((NT, 1, 128), F32),
            pltpu.VMEM((NT, 1, 128), F32),
            pltpu.SemaphoreType.DMA,
            pltpu.SemaphoreType.DMA,
            pltpu.SemaphoreType.DMA((3,)),
            pltpu.SemaphoreType.DMA((3,)),
            pltpu.SemaphoreType.DMA,
            pltpu.SemaphoreType.DMA,
            pltpu.SemaphoreType.DMA,
            pltpu.SemaphoreType.DMA,
        ],
        compiler_params=pltpu.CompilerParams(
            collective_id=0, has_side_effects=True, vmem_limit_bytes=48 * 1024 * 1024
        ),
        name="raster",
    )(attributes, cell_basin, w1, w2, w3, hw)


def bucket_kernel(sums, cells, precip, temp, pet, out):
    mean = sums[...] / cells[...].astype(F32)
    shape = (8, 128)
    param = [LOW[p] + SPAN[p] * mean[p : p + 1] for p in range(12)]
    tt, cfmax, fc, beta, lp, k0, k1, k2, uzl, perc = [
        jnp.broadcast_to(param[p], shape) for p in range(10)
    ]
    raw = [
        jnp.exp((param[10] - 1.0) * jnp.log(jnp.float32(k + 0.5)) - (k + 0.5) / param[11])
        for k in range(LAGS)
    ]
    total = raw[0]
    for k in range(1, LAGS):
        total = total + raw[k]
    kernel = [jnp.broadcast_to(r / total, shape) for r in raw]
    dry = lp * fc
    per_dry = 1.0 / dry
    per_fc = 1.0 / fc
    snow = jnp.zeros(shape, F32)
    soil = 0.5 * fc
    upper = jnp.full(shape, 5.0, F32)
    lower = jnp.full(shape, 20.0, F32)
    runoff = []
    for d in range(precip.shape[0]):
        rain, air, demand = precip[d], temp[d], pet[d]
        warm = air - tt
        liquid = jax.nn.sigmoid(warm)
        wet = rain * liquid
        gained = snow + (rain - wet)
        snow = jnp.maximum(gained - cfmax * jnp.maximum(warm, 0.0), 0.0)
        inflow = wet + (gained - snow)
        recharge = inflow * jnp.exp(beta * jnp.log(soil * per_fc))
        soil = soil + inflow - recharge
        excess = jnp.maximum(soil - fc, 0.0)
        soil = soil - excess
        soil = jnp.where(soil < dry, soil * (1.0 - demand * per_dry), soil - demand)
        upper = upper + recharge + excess
        upper_new = jnp.maximum(upper - perc, 0.0)
        lower = lower + upper - upper_new
        quick = k0 * jnp.maximum(upper_new - uzl, 0.0)
        slow = k1 * upper_new
        upper = upper_new - quick - slow
        base = k2 * lower
        lower = lower - base
        runoff.append(quick + slow + base)
        flow = kernel[0] * runoff[d]
        for k in range(1, min(d, LAGS - 1) + 1):
            flow = flow + kernel[k] * runoff[d - k]
        out[d] = flow


def bucket(sums, cells, precip, temp, pet):
    vmem = pl.BlockSpec(memory_space=pltpu.VMEM)
    return pl.pallas_call(
        bucket_kernel,
        out_shape=jax.ShapeDtypeStruct(precip.shape, F32),
        in_specs=[vmem] * 5,
        out_specs=vmem,
        name="bucket",
    )(sums, cells, precip, temp, pet)


def on_device(
    attributes, cell_basin, basin_cells, conv_first, conv_second, conv_third, head_weight,
    precip, temp, pet,
):
    sums = raster(
        attributes,
        cell_basin,
        jnp.transpose(conv_first, (1, 2, 3, 0)),
        jnp.transpose(conv_second, (1, 2, 0, 3)),
        jnp.transpose(conv_third, (1, 2, 0, 3)),
        head_weight.T,
    )
    return bucket(sums, basin_cells.reshape(1, 128), precip, temp, pet)


def solution(mesh):
    return jax.shard_map(
        on_device,
        mesh=mesh,
        in_specs=(
            P(None, "tile", None),
            P("tile", None),
            P("tile"),
            P("chan", None, None, None),
            P("chan", None, None, None),
            P("chan", None, None, None),
            P("chan", None),
            P(None, "chan", "tile"),
            P(None, "chan", "tile"),
            P(None, "chan", "tile"),
        ),
        out_specs=P(None, "chan", "tile"),
        check_vma=False,
    )
```

```python
import jax
import jax.numpy as jnp
from jax import lax
from jax.experimental import pallas as pl
from jax.experimental.pallas import tpu as pltpu
from jax.sharding import PartitionSpec as P

LAGS = 15
LOW = [-2.0, 0.5, 50.0, 1.0, 0.3, 0.05, 0.01, 0.001, 0.0, 0.5, 1.0, 0.5]
SPAN = [4.0, 5.5, 450.0, 4.0, 0.7, 0.45, 0.29, 0.099, 50.0, 5.5, 2.0, 2.5]
MESH = pl.DeviceIdType.MESH
F32 = jnp.float32
BF16 = jnp.bfloat16

A = 35
TH = 16
HALF = 8
W = 512
NT = 64
CP = 64
SUB = 16
STEP = W // SUB
WP = W + 2 * SUB


def dot(a, b):
    return jnp.dot(a, b, preferred_element_type=F32)


def dot_nt(a, b):
    return lax.dot_general(a, b, (((1,), (1,)), ((), ())), preferred_element_type=F32)


def dot_tn(a, b):
    return lax.dot_general(a, b, (((0,), (0,)), ((), ())), preferred_element_type=F32)


def put_row(dst, row, a):
    sub = lax.broadcasted_iota(jnp.int32, (SUB, a.shape[1]), 0)
    dst[row, SUB : SUB + W, :] = a.astype(BF16)
    before = jnp.where(sub == 0, 0.0, pltpu.roll(a[W - SUB :], 1, axis=0))
    after = jnp.where(sub == SUB - 1, 0.0, pltpu.roll(a[:SUB], SUB - 1, axis=0))
    dst[row, :SUB, :] = before.astype(BF16)
    dst[row, SUB + W :, :] = after.astype(BF16)


def digits(value):
    return [value // 2**k % 2 for k in (5, 4, 3, 2, 1, 0)]


def greet_order(tile):
    y1, y0, z1, z0, x1, x0 = digits(tile)
    return ((((y1 * 2 + z1) * 2 + x1) * 2 + y0) * 2 + z0) * 2 + x0


def greet_tile(place):
    y1, z1, x1, y0, z0, x0 = digits(place)
    return ((((y1 * 2 + y0) * 2 + z1) * 2 + z0) * 2 + x1) * 2 + x0


def signal(sem, **where):
    pl.semaphore_signal(sem, inc=1, device_id=where, device_id_type=MESH)


def line_peers(tile):
    lines = []
    for weight in (1, 4, 16):
        at = lax.rem(tile // weight, 4)
        lines.append([tile + (lax.rem(at + k, 4) - at) * weight for k in range(1, 4)])
    return lines


def raster_kernel(
    attr_in, cb_in, cells_in, w1_in, w2_in, w3_in, hw_in, precip_in, temp_in, pet_in, out,
    attr, cb, cells, w1, w2, w3, hw, precip, temp, pet, w1r, w2r, w3r, hwr,
    spread, slots, perm, wide1, wide2, wide3, wideh, h0, h1, h2, h3, sendb, recvb,
    local_sems, halo_send, halo_recv, w_send, w_recv, row_send, row_recv,
    z_sem, y_sem, c_sem,
):
    tile = lax.axis_index("tile")
    chan = lax.axis_index("chan")
    barrier = pltpu.get_barrier_semaphore()
    locals_ = [
        pltpu.make_async_copy(src, dst, local_sems.at[k])
        for k, (src, dst) in enumerate(
            (
                (attr_in, attr), (w1_in, w1), (hw_in, hw), (cb_in, cb), (w2_in, w2), (w3_in, w3),
                (cells_in, cells), (precip_in, precip), (temp_in, temp), (pet_in, pet),
            )
        )
    ]
    for copy in locals_:
        copy.start()
    got_attr, got_w1, got_hw, got_cb, got_w2, got_w3 = locals_[:6]

    step = jnp.where(chan == 0, 1, NT - 1)
    towards = lax.rem(tile + step, NT)
    source = lax.rem(tile + NT - step, NT)
    signal(barrier, chan=1 - chan)
    signal(barrier, tile=source)
    x_peers, z_peers, y_peers = line_peers(tile)
    for peer in x_peers + z_peers + y_peers:
        signal(barrier, tile=peer)

    place = lax.broadcasted_iota(jnp.int32, (W, W), 0)
    column = lax.broadcasted_iota(jnp.int32, (W, W), 1)
    perm[...] = ((place % SUB) * STEP + place // SUB == column).astype(F32).astype(BF16)
    wide1[...] = jnp.zeros(wide1.shape, BF16)
    wideh[...] = jnp.zeros(wideh.shape, BF16)
    for wide in (wide2, wide3):
        wide[0:128, 1152:1536] = jnp.zeros((128, 384), BF16)
        wide[128:256, 0:384] = jnp.zeros((128, 384), BF16)

    def place_rows(first, last):
        for r in range(first, last):
            for g in range(4):
                part = spread[g, pl.ds(r, 48, stride=TH), :]
                slots[(3 + r) * CP : (3 + r) * CP + 48, g * 128 : (g + 1) * 128] = part.astype(BF16)
            slots[(3 + r) * CP + 48 : (4 + r) * CP, :] = jnp.zeros((CP - 48, W), BF16)

    got_attr.wait()
    flat = attr[...].reshape(A * TH, W)
    for g in range(4):
        spread[g, : A * TH, :] = flat[:, g * 128 : (g + 1) * 128].astype(F32)
        spread[g, A * TH :, :] = jnp.zeros((48 * TH - A * TH, 128), F32)
    place_rows(0, 3)
    place_rows(13, 16)

    pl.semaphore_wait(barrier, 11)
    src_at = pl.multiple_of((16 - 13 * chan) * CP, CP)
    dst_at = pl.multiple_of(19 * chan * CP, CP)
    halo = pltpu.make_async_remote_copy(
        src_ref=slots.at[pl.ds(src_at, 3 * CP)],
        dst_ref=slots.at[pl.ds(dst_at, 3 * CP)],
        send_sem=halo_send,
        recv_sem=halo_recv,
        device_id={"tile": towards},
        device_id_type=MESH,
    )
    halo.start()
    weights = [
        pltpu.make_async_remote_copy(
            src_ref=src,
            dst_ref=dst,
            send_sem=w_send.at[k],
            recv_sem=w_recv.at[k],
            device_id={"chan": 1 - chan},
            device_id_type=MESH,
        )
        for k, (src, dst) in enumerate(((w1_in, w1r), (hw_in, hwr), (w2_in, w2r), (w3_in, w3r)))
    ]
    for copy in weights:
        copy.start()
    for peer in z_peers:
        signal(z_sem, tile=peer)
    place_rows(3, 13)

    def arrange(block, count):
        at = pl.multiple_of((chan * HALF + 2 * block) * CP, 2 * CP)
        a = dot_nt(perm[...], slots[pl.ds(at, count * 2 * CP), :])
        for k in range(count):
            put_row(h0, block + k, a[:, k * 128 : (k + 1) * 128])

    first_own = 2 * (1 - chan)
    arrange(first_own, 2)
    arrange(first_own + 2, 2)
    arrange(first_own + 4, 1)

    sub8 = lax.broadcasted_iota(jnp.int32, (HALF, 128), 0)
    lane8 = lax.broadcasted_iota(jnp.int32, (HALF, 128), 1)
    sub16 = lax.broadcasted_iota(jnp.int32, (SUB, 128), 0)
    got_cb.wait()
    own = cb[pl.ds(pl.multiple_of(chan * HALF, HALF), HALF), :]
    ids1, ids2, owners = [], [], []
    limit = jnp.zeros((SUB, 128), F32)
    for g in range(4):
        run = own[:, g * 128 : (g + 1) * 128]
        first = run[:, :1]
        last = run[:, 127:]
        count = jnp.sum((run == first).astype(F32), axis=1, keepdims=True)
        count = jnp.where(lane8 // 16 == sub8, jnp.broadcast_to(count, (HALF, 128)), 0.0)
        count = jnp.sum(count, axis=0, keepdims=True)
        limit = jnp.where(sub16 // 4 == g, jnp.broadcast_to(count, (SUB, 128)), limit)
        owners.append(first // 128)
        ids1.append((first % 128).astype(F32))
        ids2.append((last % 128).astype(F32))
    limit = limit - ((sub16 % 4) * STEP).astype(F32)

    def widen(mine, theirs, wide):
        for half, ref in ((chan, mine), (1 - chan, theirs)):
            for t in range(9):
                dy, dx = t // 3, t % 3
                w = ref[dy, dx]
                for e in range(2):
                    at = ((dy + e) * 3 + dx) * 128
                    wide[pl.ds(pl.multiple_of(e * 128 + half * 64, 64), 64), at : at + 128] = w

    def both(mine, theirs):
        left = jnp.where(chan == 0, mine, theirs)
        right = jnp.where(chan == 0, theirs, mine)
        return jnp.concatenate([left, right], axis=1)

    got_w1.wait()
    weights[0].wait_recv()
    for t in range(9):
        dy, dx = t // 3, t % 3
        w = both(w1[dy, dx].astype(F32), w1r[dy, dx].astype(F32)).astype(BF16)
        for e in range(2):
            row = dy + e
            at = ((row // 2) * 3 + dx) * 128 + (row % 2) * CP
            wide1[at : at + A, e * 128 : (e + 1) * 128] = w

    top = jnp.logical_and(chan == 0, tile == 0)
    bottom = jnp.logical_and(chan == 1, tile == NT - 1)
    halo.wait_recv()

    @pl.when(jnp.logical_or(top, bottom))
    def _():
        slots[pl.ds(dst_at, 3 * CP), :] = jnp.zeros((3 * CP, W), BF16)

    arrange(5 * chan, 2)

    for pair in range(6):
        lhs = jnp.concatenate(
            [h0[pair + b, dx * SUB : dx * SUB + W, :] for b in range(2) for dx in range(3)], axis=1
        )
        acc = jnp.maximum(dot(lhs, wide1[...]), 0.0)
        put_row(h1, 2 * pair, acc[:, :128])
        put_row(h1, 2 * pair + 1, acc[:, 128:])

    @pl.when(top)
    def _():
        h1[0:2] = jnp.zeros((2, WP, 128), BF16)

    @pl.when(bottom)
    def _():
        h1[10:12] = jnp.zeros((2, WP, 128), BF16)

    def taps(src, pair):
        return jnp.concatenate(
            [
                src[2 * pair + dy, dx * SUB : dx * SUB + W, :]
                for dy in range(4)
                for dx in range(3)
            ],
            axis=1,
        )

    pl.semaphore_wait(z_sem, 3)
    for peer in y_peers:
        signal(y_sem, tile=peer)
    got_w2.wait()
    weights[2].wait_recv()
    widen(w2, w2r, wide2)
    for pair in range(5):
        acc = jnp.maximum(dot_nt(taps(h1, pair), wide2[...]), 0.0)
        put_row(h2, 2 * pair, acc[:, :128])
        put_row(h2, 2 * pair + 1, acc[:, 128:])

    @pl.when(top)
    def _():
        h2[0:1] = jnp.zeros((1, WP, 128), BF16)

    @pl.when(bottom)
    def _():
        h2[9:10] = jnp.zeros((1, WP, 128), BF16)

    pl.semaphore_wait(y_sem, 3)
    signal(c_sem, chan=1 - chan)
    got_w3.wait()
    weights[3].wait_recv()
    widen(w3, w3r, wide3)
    for pair in range(4):
        acc = jnp.maximum(dot_nt(taps(h2, pair), wide3[...]), 0.0)
        h3[:, pair * 256 : (pair + 1) * 256] = acc.astype(BF16)

    got_hw.wait()
    weights[1].wait_recv()
    w = both(hw[...].astype(F32), hwr[...].astype(F32)).astype(BF16)
    for r in range(HALF):
        wideh[r * 16 : r * 16 + 12, r * 128 : (r + 1) * 128] = w
    share = jax.nn.sigmoid(dot_nt(h3[...], wideh[...]))
    sums = [jnp.zeros((SUB, 128), F32), jnp.zeros((SUB, 128), F32)]
    for j in range(STEP):
        v = share[j * SUB : (j + 1) * SUB]
        inside = limit > j
        sums[0] = sums[0] + jnp.where(inside, v, 0.0)
        sums[1] = sums[1] + jnp.where(inside, 0.0, v)
    rows = []
    for g in range(4):
        pair = []
        for s, ids in zip(sums, (ids1, ids2)):
            v = jnp.sum(s[4 * g : 4 * g + 4], axis=0, keepdims=True)
            v = jnp.where(lane8 // 16 == sub8, jnp.broadcast_to(v, (HALF, 128)), 0.0)
            for shift in (64, 32, 16):
                v = v + pltpu.roll(v, shift, axis=1)
            pair.append(jnp.where(lane8 % 16 == 12, jnp.broadcast_to(ids[g], (HALF, 128)), v))
        rows.append(jnp.where((lane8 // 16) % 2 == 0, pair[0], pair[1]))
    value = jnp.concatenate(rows, axis=0)
    hi = value.astype(BF16).astype(F32)
    mid = (value - hi).astype(BF16).astype(F32)
    low = value - hi - mid
    kind = lax.broadcasted_iota(jnp.int32, (32, 128), 1) // 32
    parts = jnp.where(kind == 0, hi, jnp.where(kind == 1, mid, jnp.where(kind == 2, low, 0.0)))
    to_owner = jnp.concatenate(
        [(jnp.broadcast_to(o, (HALF, 128)) == lane8).astype(F32) for o in owners], axis=0
    )
    routed = dot_tn(to_owner.astype(BF16), parts.astype(BF16))[:NT]
    sendb[...] = routed.reshape(NT, 1, 128)

    pl.semaphore_wait(c_sem, 1)
    me = chan * NT + tile
    recvb[me] = sendb[tile]
    mine_at = greet_order(tile) * 2 + chan
    for i in range(2 * NT - 1):
        swap = mine_at == i
        o = jnp.where(swap, NT - 1, greet_tile(i // 2))
        pltpu.make_async_remote_copy(
            src_ref=sendb.at[o],
            dst_ref=recvb.at[me],
            send_sem=row_send,
            recv_sem=row_recv,
            device_id={"tile": o, "chan": jnp.where(swap, 1, i % 2)},
            device_id_type=MESH,
        ).start()
    rest = pl.ds(0, 2 * NT - 1)
    pltpu.make_async_copy(recvb.at[rest], recvb.at[rest], row_recv).wait()
    got = recvb[...].reshape(2, NT, 128)
    got = got[0] + got[1]
    basin = lax.broadcasted_iota(jnp.int32, (NT, 128), 1).astype(F32)
    gotb = got.astype(BF16)
    total = jnp.zeros((16, 128), F32)
    for b in range(2):
        hit = (jnp.broadcast_to(got[:, 16 * b + 12 : 16 * b + 13], (NT, 128)) == basin).astype(F32)
        placed = dot_tn(gotb, hit.astype(BF16))
        for k in range(3):
            total = total + placed[32 * k + 16 * b : 32 * k + 16 * b + 16]

    for copy in locals_[6:]:
        copy.wait()
    bucket(total, cells[...], precip, temp, pet, out)

    pltpu.make_async_copy(recvb.at[rest], recvb.at[rest], row_send).wait()
    halo.wait_send()
    for copy in weights:
        copy.wait_send()


def bucket(sums, cells, precip, temp, pet, out):
    mean = sums / cells.astype(F32)
    shape = (8, 128)
    param = [LOW[p] + SPAN[p] * mean[p : p + 1] for p in range(12)]
    tt, cfmax, fc, beta, lp, k0, k1, k2, uzl, perc = [
        jnp.broadcast_to(param[p], shape) for p in range(10)
    ]
    raw = [
        jnp.exp((param[10] - 1.0) * jnp.log(jnp.float32(k + 0.5)) - (k + 0.5) / param[11])
        for k in range(LAGS)
    ]
    total = raw[0]
    for k in range(1, LAGS):
        total = total + raw[k]
    kernel = [jnp.broadcast_to(r / total, shape) for r in raw]
    dry = lp * fc
    per_dry = 1.0 / dry
    per_fc = 1.0 / fc
    snow = jnp.zeros(shape, F32)
    soil = 0.5 * fc
    upper = jnp.full(shape, 5.0, F32)
    lower = jnp.full(shape, 20.0, F32)
    runoff = []
    for d in range(precip.shape[0]):
        rain, air, demand = precip[d], temp[d], pet[d]
        warm = air - tt
        liquid = jax.nn.sigmoid(warm)
        wet = rain * liquid
        gained = snow + (rain - wet)
        snow = jnp.maximum(gained - cfmax * jnp.maximum(warm, 0.0), 0.0)
        inflow = wet + (gained - snow)
        recharge = inflow * jnp.exp(beta * jnp.log(soil * per_fc))
        soil = soil + inflow - recharge
        excess = jnp.maximum(soil - fc, 0.0)
        soil = soil - excess
        soil = jnp.where(soil < dry, soil * (1.0 - demand * per_dry), soil - demand)
        upper = upper + recharge + excess
        upper_new = jnp.maximum(upper - perc, 0.0)
        lower = lower + upper - upper_new
        quick = k0 * jnp.maximum(upper_new - uzl, 0.0)
        slow = k1 * upper_new
        upper = upper_new - quick - slow
        base = k2 * lower
        lower = lower - base
        runoff.append(quick + slow + base)
        flow = kernel[0] * runoff[d]
        for k in range(1, min(d, LAGS - 1) + 1):
            flow = flow + kernel[k] * runoff[d - k]
        out[d] = flow


def on_device(
    attributes, cell_basin, basin_cells, conv_first, conv_second, conv_third, head_weight,
    precip, temp, pet,
):
    args = (
        attributes,
        cell_basin,
        basin_cells.reshape(1, 128),
        jnp.transpose(conv_first, (1, 2, 3, 0)),
        jnp.transpose(conv_second, (1, 2, 0, 3)),
        jnp.transpose(conv_third, (1, 2, 0, 3)),
        head_weight.T,
        precip,
        temp,
        pet,
    )
    held = [pltpu.VMEM(a.shape, a.dtype) for a in args]
    theirs = [pltpu.VMEM(args[k].shape, BF16) for k in (3, 4, 5, 6)]
    return pl.pallas_call(
        raster_kernel,
        out_shape=jax.ShapeDtypeStruct(precip.shape, F32),
        in_specs=[pl.BlockSpec(memory_space=pltpu.HBM)] * len(args),
        out_specs=pl.BlockSpec(memory_space=pltpu.VMEM),
        scratch_shapes=held
        + theirs
        + [
            pltpu.VMEM((4, 48 * TH, 128), F32),
            pltpu.VMEM((22 * CP, W), BF16),
            pltpu.VMEM((W, W), BF16),
            pltpu.VMEM((768, 256), BF16),
            pltpu.VMEM((256, 1536), BF16),
            pltpu.VMEM((256, 1536), BF16),
            pltpu.VMEM((128, 1024), BF16),
            pltpu.VMEM((7, WP, 128), BF16),
            pltpu.VMEM((12, WP, 128), BF16),
            pltpu.VMEM((10, WP, 128), BF16),
            pltpu.VMEM((W, 1024), BF16),
            pltpu.VMEM((NT, 1, 128), F32),
            pltpu.VMEM((2 * NT, 1, 128), F32),
            pltpu.SemaphoreType.DMA((10,)),
            pltpu.SemaphoreType.DMA,
            pltpu.SemaphoreType.DMA,
            pltpu.SemaphoreType.DMA((4,)),
            pltpu.SemaphoreType.DMA((4,)),
            pltpu.SemaphoreType.DMA,
            pltpu.SemaphoreType.DMA,
            pltpu.SemaphoreType.REGULAR,
            pltpu.SemaphoreType.REGULAR,
            pltpu.SemaphoreType.REGULAR,
        ],
        compiler_params=pltpu.CompilerParams(
            collective_id=0, has_side_effects=True, vmem_limit_bytes=56 * 1024 * 1024
        ),
        name="raster",
    )(*args)


def solution(mesh):
    return jax.shard_map(
        on_device,
        mesh=mesh,
        in_specs=(
            P(None, "tile", None),
            P("tile", None),
            P("tile"),
            P("chan", None, None, None),
            P("chan", None, None, None),
            P("chan", None, None, None),
            P("chan", None),
            P(None, "chan", "tile"),
            P(None, "chan", "tile"),
            P(None, "chan", "tile"),
        ),
        out_specs=P(None, "chan", "tile"),
        check_vma=False,
    )
```

```python
import jax
import jax.numpy as jnp
from jax import lax
from jax.experimental import pallas as pl
from jax.experimental.pallas import tpu as pltpu
from jax.sharding import PartitionSpec as P

LAGS = 15
LOW = [-2.0, 0.5, 50.0, 1.0, 0.3, 0.05, 0.01, 0.001, 0.0, 0.5, 1.0, 0.5]
SPAN = [4.0, 5.5, 450.0, 4.0, 0.7, 0.45, 0.29, 0.099, 50.0, 5.5, 2.0, 2.5]
MESH = pl.DeviceIdType.MESH
F32 = jnp.float32
BF16 = jnp.bfloat16

A = 35
TH = 16
HALF = 8
W = 512
NT = 64
CP = 64
SUB = 16
STEP = W // SUB
WP = W + 2 * SUB


def dot(a, b):
    return jnp.dot(a, b, preferred_element_type=F32)


def dot_nt(a, b):
    return lax.dot_general(a, b, (((1,), (1,)), ((), ())), preferred_element_type=F32)


def dot_tn(a, b):
    return lax.dot_general(a, b, (((0,), (0,)), ((), ())), preferred_element_type=F32)


def put_row(dst, row, a):
    sub = lax.broadcasted_iota(jnp.int32, (SUB, a.shape[1]), 0)
    dst[row, SUB : SUB + W, :] = a.astype(BF16)
    before = jnp.where(sub == 0, 0.0, pltpu.roll(a[W - SUB :], 1, axis=0))
    after = jnp.where(sub == SUB - 1, 0.0, pltpu.roll(a[:SUB], SUB - 1, axis=0))
    dst[row, :SUB, :] = before.astype(BF16)
    dst[row, SUB + W :, :] = after.astype(BF16)


def put_pair(dst, pair, a, keep):
    for e in range(2):
        row = a[:, e * 128 : (e + 1) * 128]
        put_row(dst, 2 * pair + e, row if keep is None else row * keep[e])


def digits(value):
    return [value // 2**k % 2 for k in (5, 4, 3, 2, 1, 0)]


def greet_order(tile):
    y1, y0, z1, z0, x1, x0 = digits(tile)
    return ((((y1 * 2 + z1) * 2 + x1) * 2 + y0) * 2 + z0) * 2 + x0


def greet_tile(place):
    y1, z1, x1, y0, z0, x0 = digits(place)
    return ((((y1 * 2 + y0) * 2 + z1) * 2 + z0) * 2 + x1) * 2 + x0


def signal(sem, **where):
    pl.semaphore_signal(sem, inc=1, device_id=where, device_id_type=MESH)


def line_peers(tile):
    lines = []
    for weight in (1, 4, 16):
        at = lax.rem(tile // weight, 4)
        lines.append([tile + (lax.rem(at + k, 4) - at) * weight for k in range(1, 4)])
    return lines


def raster_kernel(
    attr_in, cb_in, cells_in, w1_in, w2_in, w3_in, hw_in, precip_in, temp_in, pet_in, out,
    attr, cb, cells, w1, w2, w3, hw, precip, temp, pet, w1r, w2r, w3r, hwr,
    spread, slots, perm, wide1, wide2, wide3, wideh, h0, h1, h2, h3, sendb, recvb,
    local_sems, halo_send, halo_recv, w_send, w_recv, row_send, row_recv,
    z_sem, y_sem,
):
    tile = lax.axis_index("tile")
    chan = lax.axis_index("chan")
    barrier = pltpu.get_barrier_semaphore()
    locals_ = [
        pltpu.make_async_copy(src, dst, local_sems.at[k])
        for k, (src, dst) in enumerate(
            (
                (attr_in, attr), (w1_in, w1), (hw_in, hw), (cb_in, cb), (w2_in, w2), (w3_in, w3),
                (cells_in, cells), (precip_in, precip), (temp_in, temp), (pet_in, pet),
            )
        )
    ]
    for copy in locals_:
        copy.start()
    got_attr, got_w1, got_hw, got_cb, got_w2, got_w3 = locals_[:6]

    edge = jnp.where(chan == 0, 0, NT - 1)
    far = NT - 1 - edge
    step = 1 - 2 * chan
    lacks = tile == edge
    gives = tile != far
    towards = jnp.where(gives, tile + step, tile - step)
    source = jnp.where(lacks, tile + step, tile - step)
    signal(barrier, chan=1 - chan)
    x_peers, z_peers, y_peers = line_peers(tile)

    @pl.when(jnp.logical_not(lacks))
    def _():
        signal(barrier, tile=source)

    for peer in x_peers + z_peers + y_peers:
        signal(barrier, tile=peer)

    place = lax.broadcasted_iota(jnp.int32, (W, W), 0)
    column = lax.broadcasted_iota(jnp.int32, (W, W), 1)
    perm[...] = ((place % SUB) * STEP + place // SUB == column).astype(F32).astype(BF16)
    wide1[...] = jnp.zeros(wide1.shape, BF16)
    wideh[...] = jnp.zeros(wideh.shape, BF16)
    for wide in (wide2, wide3):
        wide[0:128, 1152:1536] = jnp.zeros((128, 384), BF16)
        wide[128:256, 0:384] = jnp.zeros((128, 384), BF16)

    def place_rows(first, last):
        for i in range(first, last):
            r = jnp.where(chan == 0, i, TH - 1 - i)
            for g in range(4):
                part = spread[g, pl.ds(r, 48, stride=TH), :]
                slots[(3 + i) * CP : (3 + i) * CP + 48, g * 128 : (g + 1) * 128] = part.astype(BF16)
            slots[(3 + i) * CP + 48 : (4 + i) * CP, :] = jnp.zeros((CP - 48, W), BF16)

    pl.semaphore_wait(barrier, 10 + gives.astype(jnp.int32))
    weights = [
        pltpu.make_async_remote_copy(
            src_ref=src,
            dst_ref=dst,
            send_sem=w_send.at[k],
            recv_sem=w_recv.at[k],
            device_id={"chan": 1 - chan},
            device_id_type=MESH,
        )
        for k, (src, dst) in enumerate(((w1_in, w1r), (hw_in, hwr), (w2_in, w2r), (w3_in, w3r)))
    ]
    for copy in weights:
        copy.start()
    for peer in z_peers:
        signal(z_sem, tile=peer)

    got_attr.wait()
    flat = attr[...].reshape(A * TH, W)
    for g in range(4):
        spread[g, : A * TH, :] = flat[:, g * 128 : (g + 1) * 128].astype(F32)
        spread[g, A * TH :, :] = jnp.zeros((48 * TH - A * TH, 128), F32)
    place_rows(13, 16)
    halo = pltpu.make_async_remote_copy(
        src_ref=slots.at[pl.ds(16 * CP, 3 * CP)],
        dst_ref=slots.at[pl.ds(0, 3 * CP)],
        send_sem=halo_send,
        recv_sem=halo_recv,
        device_id={"tile": towards},
        device_id_type=MESH,
    )

    @pl.when(gives)
    def _():
        halo.start()

    @pl.when(lacks)
    def _():
        slots[: 3 * CP, :] = jnp.zeros((3 * CP, W), BF16)

    place_rows(0, 11)

    def arrange(block, count):
        at = 2 * block * CP
        a = dot_nt(perm[...], slots[at : at + count * 2 * CP, :])
        for k in range(count):
            put_row(h0, block + k, a[:, k * 128 : (k + 1) * 128])

    arrange(2, 2)
    arrange(4, 2)
    arrange(6, 1)

    sub8 = lax.broadcasted_iota(jnp.int32, (HALF, 128), 0)
    lane8 = lax.broadcasted_iota(jnp.int32, (HALF, 128), 1)
    mine8 = lane8 // 16 == jnp.where(chan == 0, sub8, HALF - 1 - sub8)
    sub16 = lax.broadcasted_iota(jnp.int32, (SUB, 128), 0)
    got_cb.wait()
    own = cb[pl.ds(pl.multiple_of(chan * HALF, HALF), HALF), :]
    ids1, ids2, owners = [], [], []
    limit = jnp.zeros((SUB, 128), F32)
    for g in range(4):
        run = own[:, g * 128 : (g + 1) * 128]
        first = run[:, :1]
        last = run[:, 127:]
        count = jnp.sum((run == first).astype(F32), axis=1, keepdims=True)
        count = jnp.where(mine8, jnp.broadcast_to(count, (HALF, 128)), 0.0)
        count = jnp.sum(count, axis=0, keepdims=True)
        limit = jnp.where(sub16 // 4 == g, jnp.broadcast_to(count, (SUB, 128)), limit)
        owners.append(first // 128)
        ids1.append((first % 128).astype(F32))
        ids2.append((last % 128).astype(F32))
    limit = limit - ((sub16 % 4) * STEP).astype(F32)

    def widen(mine, theirs, wide):
        for half, ref in ((chan, mine), (1 - chan, theirs)):
            for t in range(9):
                dy, dx = t // 3, t % 3
                w = ref[jnp.where(chan == 0, dy, 2 - dy), dx]
                for e in range(2):
                    at = ((dy + e) * 3 + dx) * 128
                    wide[pl.ds(pl.multiple_of(e * 128 + half * 64, 64), 64), at : at + 128] = w

    def both(mine, theirs):
        left = jnp.where(chan == 0, mine, theirs)
        right = jnp.where(chan == 0, theirs, mine)
        return jnp.concatenate([left, right], axis=1)

    for copy in (got_w1, got_w2, got_w3, got_hw):
        copy.wait()
    for copy in weights:
        copy.wait_recv()
    for t in range(9):
        dy, dx = t // 3, t % 3
        at = jnp.where(chan == 0, dy, 2 - dy)
        w = both(w1[at, dx].astype(F32), w1r[at, dx].astype(F32)).astype(BF16)
        for e in range(2):
            row = dy + e
            at = ((row // 2) * 3 + dx) * 128 + (row % 2) * CP
            wide1[at : at + A, e * 128 : (e + 1) * 128] = w
    widen(w2, w2r, wide2)
    widen(w3, w3r, wide3)
    w = both(hw[...].astype(F32), hwr[...].astype(F32)).astype(BF16)
    for r in range(HALF):
        wideh[r * 16 : r * 16 + 12, r * 128 : (r + 1) * 128] = w

    def taps(src, pair):
        return jnp.concatenate(
            [
                src[2 * pair + dy, dx * SUB : dx * SUB + W, :]
                for dy in range(4)
                for dx in range(3)
            ],
            axis=1,
        )

    def conv1(pair, keep=None):
        lhs = jnp.concatenate(
            [h0[pair + b, dx * SUB : dx * SUB + W, :] for b in range(2) for dx in range(3)], axis=1
        )
        put_pair(h1, pair, jnp.maximum(dot(lhs, wide1[...]), 0.0), keep)

    def conv2(pair, keep=None):
        put_pair(h2, pair, jnp.maximum(dot_nt(taps(h1, pair), wide2[...]), 0.0), keep)

    def conv3(pair):
        h3[pair] = jnp.maximum(dot_nt(taps(h2, pair), wide3[...]), 0.0).astype(BF16)

    for pair in range(2, 6):
        conv1(pair)
    for pair in range(2, 5):
        conv2(pair)
    pl.semaphore_wait(z_sem, 3)
    for peer in y_peers:
        signal(y_sem, tile=peer)
        signal(y_sem, tile=peer, chan=1 - chan)
    signal(y_sem, chan=1 - chan)
    for pair in range(2, 4):
        conv3(pair)

    @pl.when(jnp.logical_not(lacks))
    def _():
        halo.wait_recv()

    arrange(0, 2)
    inside = 1.0 - lacks.astype(F32)
    conv1(1)
    conv1(0, (inside, inside))
    conv2(1)
    conv2(0, (inside, 1.0))
    conv3(1)
    conv3(0)

    share = jax.nn.sigmoid(
        dot_nt(jnp.concatenate([h3[q] for q in range(4)], axis=1), wideh[...])
    )
    sums = [jnp.zeros((SUB, 128), F32), jnp.zeros((SUB, 128), F32)]
    for j in range(STEP):
        v = share[j * SUB : (j + 1) * SUB]
        inside = limit > j
        sums[0] = sums[0] + jnp.where(inside, v, 0.0)
        sums[1] = sums[1] + jnp.where(inside, 0.0, v)
    rows = []
    for g in range(4):
        pair = []
        for s, ids in zip(sums, (ids1, ids2)):
            v = jnp.sum(s[4 * g : 4 * g + 4], axis=0, keepdims=True)
            v = jnp.where(mine8, jnp.broadcast_to(v, (HALF, 128)), 0.0)
            for shift in (64, 32, 16):
                v = v + pltpu.roll(v, shift, axis=1)
            pair.append(jnp.where(lane8 % 16 == 12, jnp.broadcast_to(ids[g], (HALF, 128)), v))
        rows.append(jnp.where((lane8 // 16) % 2 == 0, pair[0], pair[1]))
    value = jnp.concatenate(rows, axis=0)
    hi = value.astype(BF16).astype(F32)
    mid = (value - hi).astype(BF16).astype(F32)
    low = value - hi - mid
    kind = lax.broadcasted_iota(jnp.int32, (32, 128), 1) // 32
    parts = jnp.where(kind == 0, hi, jnp.where(kind == 1, mid, jnp.where(kind == 2, low, 0.0)))
    to_owner = jnp.concatenate(
        [(jnp.broadcast_to(o, (HALF, 128)) == lane8).astype(F32) for o in owners], axis=0
    )
    routed = dot_tn(to_owner.astype(BF16), parts.astype(BF16))[:NT]
    sendb[...] = routed.reshape(NT, 1, 128)

    pl.semaphore_wait(y_sem, 7)
    me = chan * NT + tile
    recvb[me] = sendb[tile]
    mine_at = greet_order(tile) * 2 + chan
    for i in range(2 * NT - 1):
        swap = mine_at == i
        o = jnp.where(swap, NT - 1, greet_tile(i // 2))
        pltpu.make_async_remote_copy(
            src_ref=sendb.at[o],
            dst_ref=recvb.at[me],
            send_sem=row_send,
            recv_sem=row_recv,
            device_id={"tile": o, "chan": jnp.where(swap, 1, i % 2)},
            device_id_type=MESH,
        ).start()
    rest = pl.ds(0, 2 * NT - 1)
    pltpu.make_async_copy(recvb.at[rest], recvb.at[rest], row_recv).wait()
    got = recvb[...].reshape(2, NT, 128)
    got = got[0] + got[1]
    basin = lax.broadcasted_iota(jnp.int32, (NT, 128), 1).astype(F32)
    gotb = got.astype(BF16)
    total = jnp.zeros((16, 128), F32)
    for b in range(2):
        hit = (jnp.broadcast_to(got[:, 16 * b + 12 : 16 * b + 13], (NT, 128)) == basin).astype(F32)
        placed = dot_tn(gotb, hit.astype(BF16))
        for k in range(3):
            total = total + placed[32 * k + 16 * b : 32 * k + 16 * b + 16]

    for copy in locals_[6:]:
        copy.wait()
    bucket(total, cells[...], precip, temp, pet, out)

    pltpu.make_async_copy(recvb.at[rest], recvb.at[rest], row_send).wait()

    @pl.when(gives)
    def _():
        halo.wait_send()

    for copy in weights:
        copy.wait_send()


def bucket(sums, cells, precip, temp, pet, out):
    mean = sums / cells.astype(F32)
    shape = (8, 128)
    param = [LOW[p] + SPAN[p] * mean[p : p + 1] for p in range(12)]
    tt, cfmax, fc, beta, lp, k0, k1, k2, uzl, perc = [
        jnp.broadcast_to(param[p], shape) for p in range(10)
    ]
    raw = [
        jnp.exp((param[10] - 1.0) * jnp.log(jnp.float32(k + 0.5)) - (k + 0.5) / param[11])
        for k in range(LAGS)
    ]
    total = raw[0]
    for k in range(1, LAGS):
        total = total + raw[k]
    kernel = [jnp.broadcast_to(r / total, shape) for r in raw]
    dry = lp * fc
    per_dry = 1.0 / dry
    per_fc = 1.0 / fc
    snow = jnp.zeros(shape, F32)
    soil = 0.5 * fc
    upper = jnp.full(shape, 5.0, F32)
    lower = jnp.full(shape, 20.0, F32)
    runoff = []
    for d in range(precip.shape[0]):
        rain, air, demand = precip[d], temp[d], pet[d]
        warm = air - tt
        liquid = jax.nn.sigmoid(warm)
        wet = rain * liquid
        gained = snow + (rain - wet)
        snow = jnp.maximum(gained - cfmax * jnp.maximum(warm, 0.0), 0.0)
        inflow = wet + (gained - snow)
        recharge = inflow * jnp.exp(beta * jnp.log(soil * per_fc))
        soil = soil + inflow - recharge
        excess = jnp.maximum(soil - fc, 0.0)
        soil = soil - excess
        soil = jnp.where(soil < dry, soil * (1.0 - demand * per_dry), soil - demand)
        upper = upper + recharge + excess
        upper_new = jnp.maximum(upper - perc, 0.0)
        lower = lower + upper - upper_new
        quick = k0 * jnp.maximum(upper_new - uzl, 0.0)
        slow = k1 * upper_new
        upper = upper_new - quick - slow
        base = k2 * lower
        lower = lower - base
        runoff.append(quick + slow + base)
        flow = kernel[0] * runoff[d]
        for k in range(1, min(d, LAGS - 1) + 1):
            flow = flow + kernel[k] * runoff[d - k]
        out[d] = flow


def on_device(
    attributes, cell_basin, basin_cells, conv_first, conv_second, conv_third, head_weight,
    precip, temp, pet,
):
    args = (
        attributes,
        cell_basin,
        basin_cells.reshape(1, 128),
        jnp.transpose(conv_first, (1, 2, 3, 0)),
        jnp.transpose(conv_second, (1, 2, 0, 3)),
        jnp.transpose(conv_third, (1, 2, 0, 3)),
        head_weight.T,
        precip,
        temp,
        pet,
    )
    held = [pltpu.VMEM(a.shape, a.dtype) for a in args]
    theirs = [pltpu.VMEM(args[k].shape, BF16) for k in (3, 4, 5, 6)]
    return pl.pallas_call(
        raster_kernel,
        out_shape=jax.ShapeDtypeStruct(precip.shape, F32),
        in_specs=[pl.BlockSpec(memory_space=pltpu.HBM)] * len(args),
        out_specs=pl.BlockSpec(memory_space=pltpu.VMEM),
        scratch_shapes=held
        + theirs
        + [
            pltpu.VMEM((4, 48 * TH, 128), F32),
            pltpu.VMEM((19 * CP, W), BF16),
            pltpu.VMEM((W, W), BF16),
            pltpu.VMEM((768, 256), BF16),
            pltpu.VMEM((256, 1536), BF16),
            pltpu.VMEM((256, 1536), BF16),
            pltpu.VMEM((128, 1024), BF16),
            pltpu.VMEM((7, WP, 128), BF16),
            pltpu.VMEM((12, WP, 128), BF16),
            pltpu.VMEM((10, WP, 128), BF16),
            pltpu.VMEM((4, W, 256), BF16),
            pltpu.VMEM((NT, 1, 128), F32),
            pltpu.VMEM((2 * NT, 1, 128), F32),
            pltpu.SemaphoreType.DMA((10,)),
            pltpu.SemaphoreType.DMA,
            pltpu.SemaphoreType.DMA,
            pltpu.SemaphoreType.DMA((4,)),
            pltpu.SemaphoreType.DMA((4,)),
            pltpu.SemaphoreType.DMA,
            pltpu.SemaphoreType.DMA,
            pltpu.SemaphoreType.REGULAR,
            pltpu.SemaphoreType.REGULAR,
        ],
        compiler_params=pltpu.CompilerParams(
            collective_id=0, has_side_effects=True, vmem_limit_bytes=56 * 1024 * 1024
        ),
        name="raster",
    )(*args)


def solution(mesh):
    return jax.shard_map(
        on_device,
        mesh=mesh,
        in_specs=(
            P(None, "tile", None),
            P("tile", None),
            P("tile"),
            P("chan", None, None, None),
            P("chan", None, None, None),
            P("chan", None, None, None),
            P("chan", None),
            P(None, "chan", "tile"),
            P(None, "chan", "tile"),
            P(None, "chan", "tile"),
        ),
        out_specs=P(None, "chan", "tile"),
        check_vma=False,
    )
```

```python
import jax
import jax.numpy as jnp
from jax import lax
from jax.experimental import pallas as pl
from jax.experimental.pallas import tpu as pltpu
from jax.sharding import PartitionSpec as P

LAGS = 15
LOW = [-2.0, 0.5, 50.0, 1.0, 0.3, 0.05, 0.01, 0.001, 0.0, 0.5, 1.0, 0.5]
SPAN = [4.0, 5.5, 450.0, 4.0, 0.7, 0.45, 0.29, 0.099, 50.0, 5.5, 2.0, 2.5]
MESH = pl.DeviceIdType.MESH
F32 = jnp.float32
BF16 = jnp.bfloat16

A = 35
TH = 16
HALF = 8
W = 512
NT = 64
GAP = TH + 1
CP = 64
SUB = 16
STEP = W // SUB
WP = W + 2 * SUB


def dot(a, b):
    return jnp.dot(a, b, preferred_element_type=F32)


def dot_nt(a, b):
    return lax.dot_general(a, b, (((1,), (1,)), ((), ())), preferred_element_type=F32)


def dot_tn(a, b):
    return lax.dot_general(a, b, (((0,), (0,)), ((), ())), preferred_element_type=F32)


def put_row(dst, row, a):
    sub = lax.broadcasted_iota(jnp.int32, (SUB, a.shape[1]), 0)
    dst[row, SUB : SUB + W, :] = a.astype(BF16)
    before = jnp.where(sub == 0, 0.0, pltpu.roll(a[W - SUB :], 1, axis=0))
    after = jnp.where(sub == SUB - 1, 0.0, pltpu.roll(a[:SUB], SUB - 1, axis=0))
    dst[row, :SUB, :] = before.astype(BF16)
    dst[row, SUB + W :, :] = after.astype(BF16)


def put_pair(dst, pair, a, keep):
    for e in range(2):
        row = a[:, e * 128 : (e + 1) * 128]
        put_row(dst, 2 * pair + e, row if keep is None else row * keep[e])


def digits(value):
    return [value // 2**k % 2 for k in (5, 4, 3, 2, 1, 0)]


def greet_order(tile):
    y1, y0, z1, z0, x1, x0 = digits(tile)
    return ((((y1 * 2 + z1) * 2 + x1) * 2 + y0) * 2 + z0) * 2 + x0


def greet_tile(place):
    y1, z1, x1, y0, z0, x0 = digits(place)
    return ((((y1 * 2 + y0) * 2 + z1) * 2 + z0) * 2 + x1) * 2 + x0


def signal(sem, **where):
    pl.semaphore_signal(sem, inc=1, device_id=where, device_id_type=MESH)


LINES = (1, 4, 16)


def signal_line(sem, tile, weights, way):
    for weight in weights:
        at = lax.rem(tile // weight, 4)
        for k in range(1, 4):

            @pl.when(at + k < 4 if way > 0 else at >= k)
            def _():
                signal(sem, tile=tile + way * k * weight)


def raster_kernel(
    attr_in, cb_in, cells_in, w1_in, w2_in, w3_in, hw_in, precip_in, temp_in, pet_in, out,
    attr, cb, cells, w1, w2, w3, hw, precip, temp, pet, w1r, w2r, w3r, hwr,
    spread, slots, perm, wide1, wide2, wide3, wideh, h0, h1, h2, h3, sendb, recvb,
    local_sems, halo_send, halo_recv, w_send, w_recv, row_send, row_recv,
    line_sem, z_sem, y_sem,
):
    tile = lax.axis_index("tile")
    chan = lax.axis_index("chan")
    barrier = pltpu.get_barrier_semaphore()
    locals_ = [
        pltpu.make_async_copy(src, dst, local_sems.at[k])
        for k, (src, dst) in enumerate(
            (
                (attr_in, attr), (w1_in, w1), (hw_in, hw), (cb_in, cb), (w2_in, w2), (w3_in, w3),
                (cells_in, cells), (precip_in, precip), (temp_in, temp), (pet_in, pet),
            )
        )
    ]
    for copy in locals_:
        copy.start()
    got_attr, got_w1, got_hw, got_cb, got_w2, got_w3 = locals_[:6]

    edge = jnp.where(chan == 0, 0, NT - 1)
    far = NT - 1 - edge
    step = 1 - 2 * chan
    lacks = tile == edge
    gives = tile != far
    towards = jnp.where(gives, tile + step, tile - step)
    source = jnp.where(lacks, tile + step, tile - step)
    signal(barrier, chan=1 - chan)
    coords = [lax.rem(tile // weight, 4) for weight in LINES]
    earlier = coords[0] + coords[1] + coords[2]
    late_half = coords[2] // 2

    @pl.when(jnp.logical_not(lacks))
    def _():
        signal(barrier, tile=source)

    signal_line(barrier, tile, LINES, 1)

    place = lax.broadcasted_iota(jnp.int32, (W, W), 0)
    column = lax.broadcasted_iota(jnp.int32, (W, W), 1)
    perm[...] = ((place % SUB) * STEP + place // SUB == column).astype(F32).astype(BF16)
    wide1[...] = jnp.zeros(wide1.shape, BF16)
    wideh[...] = jnp.zeros(wideh.shape, BF16)
    for g in range(4):
        spread[g, A * GAP :, :] = jnp.zeros((48 * GAP - A * GAP, 128), F32)
    for wide in (wide2, wide3):
        wide[0:128, 1152:1536] = jnp.zeros((128, 384), BF16)
        wide[128:256, 0:384] = jnp.zeros((128, 384), BF16)

    def place_rows(first, last):
        for i in range(first, last):
            r = jnp.where(chan == 0, i, TH - 1 - i)
            for g in range(4):
                part = spread[g, pl.ds(r, 48, stride=GAP), :]
                slots[(3 + i) * CP : (3 + i) * CP + 48, g * 128 : (g + 1) * 128] = part.astype(BF16)
            slots[(3 + i) * CP + 48 : (4 + i) * CP, :] = jnp.zeros((CP - 48, W), BF16)

    got_attr.wait()
    for c in range(A):
        field = attr[c].astype(F32)
        for g in range(4):
            spread[g, c * GAP : c * GAP + TH, :] = field[:, g * 128 : (g + 1) * 128]
    place_rows(13, 16)

    pl.semaphore_wait(barrier, 1 + earlier + gives.astype(jnp.int32))
    weights = [
        pltpu.make_async_remote_copy(
            src_ref=src,
            dst_ref=dst,
            send_sem=w_send.at[k],
            recv_sem=w_recv.at[k],
            device_id={"chan": 1 - chan},
            device_id_type=MESH,
        )
        for k, (src, dst) in enumerate(((w1_in, w1r), (hw_in, hwr), (w2_in, w2r), (w3_in, w3r)))
    ]
    for copy in weights:
        copy.start()
    halos = [
        pltpu.make_async_remote_copy(
            src_ref=slots.at[pl.ds((16 + k) * CP, 48)],
            dst_ref=slots.at[pl.ds(k * CP, 48)],
            send_sem=halo_send.at[k],
            recv_sem=halo_recv.at[k],
            device_id={"tile": towards},
            device_id_type=MESH,
        )
        for k in range(3)
    ]

    @pl.when(gives)
    def _():
        for copy in halos:
            copy.start()

    signal_line(line_sem, tile, LINES, -1)
    for k in range(3):
        slots[k * CP + 48 : (k + 1) * CP, :] = jnp.zeros((CP - 48, W), BF16)

    @pl.when(lacks)
    def _():
        for k in range(3):
            slots[k * CP : k * CP + 48, :] = jnp.zeros((48, W), BF16)

    place_rows(0, 11)

    def arrange(block, count):
        at = 2 * block * CP
        a = dot_nt(perm[...], slots[at : at + count * 2 * CP, :])
        for k in range(count):
            put_row(h0, block + k, a[:, k * 128 : (k + 1) * 128])

    arrange(2, 2)
    arrange(4, 2)
    arrange(6, 1)


    @pl.when(earlier < 9)
    def _():
        pl.semaphore_wait(line_sem, 9 - earlier)

    for k in range(1, 4):
        signal(z_sem, tile=tile + (lax.rem(coords[1] + k, 4) - coords[1]) * 4)

    sub8 = lax.broadcasted_iota(jnp.int32, (HALF, 128), 0)
    lane8 = lax.broadcasted_iota(jnp.int32, (HALF, 128), 1)
    mine8 = lane8 // 16 == jnp.where(chan == 0, sub8, HALF - 1 - sub8)
    sub16 = lax.broadcasted_iota(jnp.int32, (SUB, 128), 0)
    got_cb.wait()
    own = cb[pl.ds(pl.multiple_of(chan * HALF, HALF), HALF), :]
    ids1, ids2, owners = [], [], []
    limit = jnp.zeros((SUB, 128), F32)
    for g in range(4):
        run = own[:, g * 128 : (g + 1) * 128]
        first = run[:, :1]
        last = run[:, 127:]
        count = jnp.sum((run == first).astype(F32), axis=1, keepdims=True)
        count = jnp.where(mine8, jnp.broadcast_to(count, (HALF, 128)), 0.0)
        count = jnp.sum(count, axis=0, keepdims=True)
        limit = jnp.where(sub16 // 4 == g, jnp.broadcast_to(count, (SUB, 128)), limit)
        owners.append(first // 128)
        ids1.append((first % 128).astype(F32))
        ids2.append((last % 128).astype(F32))
    limit = limit - ((sub16 % 4) * STEP).astype(F32)

    def widen(mine, theirs, wide):
        for half, ref in ((chan, mine), (1 - chan, theirs)):
            for t in range(9):
                dy, dx = t // 3, t % 3
                w = ref[jnp.where(chan == 0, dy, 2 - dy), dx]
                for e in range(2):
                    at = ((dy + e) * 3 + dx) * 128
                    wide[pl.ds(pl.multiple_of(e * 128 + half * 64, 64), 64), at : at + 128] = w

    def both(mine, theirs):
        left = jnp.where(chan == 0, mine, theirs)
        right = jnp.where(chan == 0, theirs, mine)
        return jnp.concatenate([left, right], axis=1)

    for copy in (got_w1, got_w2, got_w3, got_hw):
        copy.wait()
    for copy in weights:
        copy.wait_recv()
    for t in range(9):
        dy, dx = t // 3, t % 3
        at = jnp.where(chan == 0, dy, 2 - dy)
        w = both(w1[at, dx].astype(F32), w1r[at, dx].astype(F32)).astype(BF16)
        for e in range(2):
            row = dy + e
            at = ((row // 2) * 3 + dx) * 128 + (row % 2) * CP
            wide1[at : at + A, e * 128 : (e + 1) * 128] = w
    widen(w2, w2r, wide2)
    widen(w3, w3r, wide3)
    w = both(hw[...].astype(F32), hwr[...].astype(F32)).astype(BF16)
    for r in range(HALF):
        wideh[r * 16 : r * 16 + 12, r * 128 : (r + 1) * 128] = w

    def taps(src, pair):
        return jnp.concatenate(
            [
                src[2 * pair + dy, dx * SUB : dx * SUB + W, :]
                for dy in range(4)
                for dx in range(3)
            ],
            axis=1,
        )

    def conv1(pair, keep=None):
        lhs = jnp.concatenate(
            [h0[pair + b, dx * SUB : dx * SUB + W, :] for b in range(2) for dx in range(3)], axis=1
        )
        put_pair(h1, pair, jnp.maximum(dot(lhs, wide1[...]), 0.0), keep)

    def conv2(pair, keep=None):
        put_pair(h2, pair, jnp.maximum(dot_nt(taps(h1, pair), wide2[...]), 0.0), keep)

    def conv3(pair):
        h3[pair] = jnp.maximum(dot_nt(taps(h2, pair), wide3[...]), 0.0).astype(BF16)

    for pair in range(2, 6):
        conv1(pair)
    for pair in range(2, 5):
        conv2(pair)
    pl.semaphore_wait(z_sem, 3)
    for k in range(1, 4):
        peer = tile + (lax.rem(coords[2] + k, 4) - coords[2]) * 16
        signal(y_sem.at[late_half], tile=peer)
        signal(y_sem.at[late_half], tile=peer, chan=1 - chan)
    signal(y_sem.at[late_half], chan=1 - chan)
    for pair in range(2, 4):
        conv3(pair)

    @pl.when(jnp.logical_not(lacks))
    def _():
        for copy in halos:
            copy.wait_recv()

    arrange(0, 2)
    inside = 1.0 - lacks.astype(F32)
    conv1(1)
    conv1(0, (inside, inside))
    conv2(1)
    conv2(0, (inside, 1.0))
    conv3(1)
    conv3(0)

    share = jax.nn.sigmoid(
        dot_nt(jnp.concatenate([h3[q] for q in range(4)], axis=1), wideh[...])
    )
    sums = [jnp.zeros((SUB, 128), F32), jnp.zeros((SUB, 128), F32)]
    for j in range(STEP):
        v = share[j * SUB : (j + 1) * SUB]
        inside = limit > j
        sums[0] = sums[0] + jnp.where(inside, v, 0.0)
        sums[1] = sums[1] + jnp.where(inside, 0.0, v)
    rows = []
    for g in range(4):
        pair = []
        for s, ids in zip(sums, (ids1, ids2)):
            v = jnp.sum(s[4 * g : 4 * g + 4], axis=0, keepdims=True)
            v = jnp.where(mine8, jnp.broadcast_to(v, (HALF, 128)), 0.0)
            for shift in (64, 32, 16):
                v = v + pltpu.roll(v, shift, axis=1)
            pair.append(jnp.where(lane8 % 16 == 12, jnp.broadcast_to(ids[g], (HALF, 128)), v))
        rows.append(jnp.where((lane8 // 16) % 2 == 0, pair[0], pair[1]))
    value = jnp.concatenate(rows, axis=0)
    hi = value.astype(BF16).astype(F32)
    mid = (value - hi).astype(BF16).astype(F32)
    low = value - hi - mid
    kind = lax.broadcasted_iota(jnp.int32, (32, 128), 1) // 32
    parts = jnp.where(kind == 0, hi, jnp.where(kind == 1, mid, jnp.where(kind == 2, low, 0.0)))
    to_owner = jnp.concatenate(
        [(jnp.broadcast_to(o, (HALF, 128)) == lane8).astype(F32) for o in owners], axis=0
    )
    routed = dot_tn(to_owner.astype(BF16), parts.astype(BF16))[:NT]
    sendb[...] = routed.reshape(NT, 1, 128)

    me = chan * NT + tile
    recvb[me] = sendb[tile]
    mine_at = greet_order(tile) * 2 + chan

    def send_row(o, c):
        pltpu.make_async_remote_copy(
            src_ref=sendb.at[o],
            dst_ref=recvb.at[me],
            send_sem=row_send,
            recv_sem=row_recv,
            device_id={"tile": o, "chan": c},
            device_id_type=MESH,
        ).start()

    for half in range(2):
        pl.semaphore_wait(y_sem.at[half], jnp.where(late_half == half, 3, 4))
        last = (half + 1) * NT - 1
        for i in range(half * NT, last):
            swap = mine_at == i
            o = jnp.where(swap, greet_tile(last // 2), greet_tile(i // 2))
            send_row(o, jnp.where(swap, last % 2, i % 2))

        @pl.when(late_half != half)
        def _():
            send_row(greet_tile(last // 2), last % 2)

    rest = pl.ds(0, 2 * NT - 1)
    pltpu.make_async_copy(recvb.at[rest], recvb.at[rest], row_recv).wait()
    got = recvb[...].reshape(2, NT, 128)
    got = got[0] + got[1]
    basin = lax.broadcasted_iota(jnp.int32, (NT, 128), 1).astype(F32)
    gotb = got.astype(BF16)
    total = jnp.zeros((16, 128), F32)
    for b in range(2):
        hit = (jnp.broadcast_to(got[:, 16 * b + 12 : 16 * b + 13], (NT, 128)) == basin).astype(F32)
        placed = dot_tn(gotb, hit.astype(BF16))
        for k in range(3):
            total = total + placed[32 * k + 16 * b : 32 * k + 16 * b + 16]

    for copy in locals_[6:]:
        copy.wait()
    bucket(total, cells[...], precip, temp, pet, out)

    pltpu.make_async_copy(recvb.at[rest], recvb.at[rest], row_send).wait()

    @pl.when(gives)
    def _():
        for copy in halos:
            copy.wait_send()

    for copy in weights:
        copy.wait_send()


def bucket(sums, cells, precip, temp, pet, out):
    mean = sums / cells.astype(F32)
    shape = (8, 128)
    param = [LOW[p] + SPAN[p] * mean[p : p + 1] for p in range(12)]
    tt, cfmax, fc, beta, lp, k0, k1, k2, uzl, perc = [
        jnp.broadcast_to(param[p], shape) for p in range(10)
    ]
    raw = [
        jnp.exp((param[10] - 1.0) * jnp.log(jnp.float32(k + 0.5)) - (k + 0.5) / param[11])
        for k in range(LAGS)
    ]
    total = raw[0]
    for k in range(1, LAGS):
        total = total + raw[k]
    kernel = [jnp.broadcast_to(r / total, shape) for r in raw]
    dry = lp * fc
    per_dry = 1.0 / dry
    per_fc = 1.0 / fc
    snow = jnp.zeros(shape, F32)
    soil = 0.5 * fc
    upper = jnp.full(shape, 5.0, F32)
    lower = jnp.full(shape, 20.0, F32)
    runoff = []
    for d in range(precip.shape[0]):
        rain, air, demand = precip[d], temp[d], pet[d]
        warm = air - tt
        liquid = jax.nn.sigmoid(warm)
        wet = rain * liquid
        gained = snow + (rain - wet)
        snow = jnp.maximum(gained - cfmax * jnp.maximum(warm, 0.0), 0.0)
        inflow = wet + (gained - snow)
        recharge = inflow * jnp.exp(beta * jnp.log(soil * per_fc))
        soil = soil + inflow - recharge
        excess = jnp.maximum(soil - fc, 0.0)
        soil = soil - excess
        soil = jnp.where(soil < dry, soil * (1.0 - demand * per_dry), soil - demand)
        upper = upper + recharge + excess
        upper_new = jnp.maximum(upper - perc, 0.0)
        lower = lower + upper - upper_new
        quick = k0 * jnp.maximum(upper_new - uzl, 0.0)
        slow = k1 * upper_new
        upper = upper_new - quick - slow
        base = k2 * lower
        lower = lower - base
        runoff.append(quick + slow + base)
        flow = kernel[0] * runoff[d]
        for k in range(1, min(d, LAGS - 1) + 1):
            flow = flow + kernel[k] * runoff[d - k]
        out[d] = flow


def on_device(
    attributes, cell_basin, basin_cells, conv_first, conv_second, conv_third, head_weight,
    precip, temp, pet,
):
    args = (
        attributes,
        cell_basin,
        basin_cells.reshape(1, 128),
        jnp.transpose(conv_first, (1, 2, 3, 0)),
        jnp.transpose(conv_second, (1, 2, 0, 3)),
        jnp.transpose(conv_third, (1, 2, 0, 3)),
        head_weight.T,
        precip,
        temp,
        pet,
    )
    held = [pltpu.VMEM(a.shape, a.dtype) for a in args]
    theirs = [pltpu.VMEM(args[k].shape, BF16) for k in (3, 4, 5, 6)]
    return pl.pallas_call(
        raster_kernel,
        out_shape=jax.ShapeDtypeStruct(precip.shape, F32),
        in_specs=[pl.BlockSpec(memory_space=pltpu.HBM)] * len(args),
        out_specs=pl.BlockSpec(memory_space=pltpu.VMEM),
        scratch_shapes=held
        + theirs
        + [
            pltpu.VMEM((4, 48 * GAP, 128), F32),
            pltpu.VMEM((19 * CP, W), BF16),
            pltpu.VMEM((W, W), BF16),
            pltpu.VMEM((768, 256), BF16),
            pltpu.VMEM((256, 1536), BF16),
            pltpu.VMEM((256, 1536), BF16),
            pltpu.VMEM((128, 1024), BF16),
            pltpu.VMEM((7, WP, 128), BF16),
            pltpu.VMEM((12, WP, 128), BF16),
            pltpu.VMEM((10, WP, 128), BF16),
            pltpu.VMEM((4, W, 256), BF16),
            pltpu.VMEM((NT, 1, 128), F32),
            pltpu.VMEM((2 * NT, 1, 128), F32),
            pltpu.SemaphoreType.DMA((10,)),
            pltpu.SemaphoreType.DMA((3,)),
            pltpu.SemaphoreType.DMA((3,)),
            pltpu.SemaphoreType.DMA((4,)),
            pltpu.SemaphoreType.DMA((4,)),
            pltpu.SemaphoreType.DMA,
            pltpu.SemaphoreType.DMA,
            pltpu.SemaphoreType.REGULAR,
            pltpu.SemaphoreType.REGULAR,
            pltpu.SemaphoreType.REGULAR((2,)),
        ],
        compiler_params=pltpu.CompilerParams(
            collective_id=0, has_side_effects=True, vmem_limit_bytes=56 * 1024 * 1024
        ),
        name="raster",
    )(*args)


def solution(mesh):
    return jax.shard_map(
        on_device,
        mesh=mesh,
        in_specs=(
            P(None, "tile", None),
            P("tile", None),
            P("tile"),
            P("chan", None, None, None),
            P("chan", None, None, None),
            P("chan", None, None, None),
            P("chan", None),
            P(None, "chan", "tile"),
            P(None, "chan", "tile"),
            P(None, "chan", "tile"),
        ),
        out_specs=P(None, "chan", "tile"),
        check_vma=False,
    )
```

```python
import jax
import jax.numpy as jnp
from jax import lax
from jax.experimental import pallas as pl
from jax.experimental.pallas import tpu as pltpu
from jax.sharding import PartitionSpec as P

LAGS = 15
LOW = [-2.0, 0.5, 50.0, 1.0, 0.3, 0.05, 0.01, 0.001, 0.0, 0.5, 1.0, 0.5]
SPAN = [4.0, 5.5, 450.0, 4.0, 0.7, 0.45, 0.29, 0.099, 50.0, 5.5, 2.0, 2.5]
MESH = pl.DeviceIdType.MESH
F32 = jnp.float32
BF16 = jnp.bfloat16

A = 35
TH = 16
HALF = 8
W = 512
NT = 64
GAP = TH + 1
CP = 64
SUB = 16
STEP = W // SUB
WP = W + 2 * SUB


def dot(a, b):
    return jnp.dot(a, b, preferred_element_type=F32)


def dot_nt(a, b):
    return lax.dot_general(a, b, (((1,), (1,)), ((), ())), preferred_element_type=F32)


def dot_tn(a, b):
    return lax.dot_general(a, b, (((0,), (0,)), ((), ())), preferred_element_type=F32)


def put_row(dst, row, a):
    sub = lax.broadcasted_iota(jnp.int32, (SUB, a.shape[1]), 0)
    dst[row, SUB : SUB + W, :] = a.astype(BF16)
    before = jnp.where(sub == 0, 0.0, pltpu.roll(a[W - SUB :], 1, axis=0))
    after = jnp.where(sub == SUB - 1, 0.0, pltpu.roll(a[:SUB], SUB - 1, axis=0))
    dst[row, :SUB, :] = before.astype(BF16)
    dst[row, SUB + W :, :] = after.astype(BF16)


def put_pair(dst, pair, a, keep):
    for e in range(2):
        row = a[:, e * 128 : (e + 1) * 128]
        put_row(dst, 2 * pair + e, row if keep is None else row * keep[e])


def digits(value):
    return [value // 2**k % 2 for k in (5, 4, 3, 2, 1, 0)]


def greet_order(tile):
    y1, y0, z1, z0, x1, x0 = digits(tile)
    return ((((y1 * 2 + z1) * 2 + x1) * 2 + y0) * 2 + z0) * 2 + x0


def greet_tile(place):
    y1, z1, x1, y0, z0, x0 = digits(place)
    return ((((y1 * 2 + y0) * 2 + z1) * 2 + z0) * 2 + x1) * 2 + x0


def signal(sem, **where):
    pl.semaphore_signal(sem, inc=1, device_id=where, device_id_type=MESH)


LINES = (1, 4, 16)


def signal_line(sem, tile, weights, way):
    for weight in weights:
        at = lax.rem(tile // weight, 4)
        for k in range(1, 4):

            @pl.when(at + k < 4 if way > 0 else at >= k)
            def _():
                signal(sem, tile=tile + way * k * weight)


def raster_kernel(
    attr_in, cb_in, cells_in, w1_in, w2_in, w3_in, hw_in, precip_in, temp_in, pet_in, out,
    attr, cb, cells, w1, w2, w3, hw, precip, temp, pet, w1r, w2r, w3r, hwr,
    spread, slots, perm, wide1, wide2, wide3, wideh, h0, h1, h2, h3, sendb, recvb,
    local_sems, halo_send, halo_recv, w_send, w_recv, row_send, row_recv,
    line_sem, z_sem, y_sem,
):
    tile = lax.axis_index("tile")
    chan = lax.axis_index("chan")
    barrier = pltpu.get_barrier_semaphore()
    locals_ = [
        pltpu.make_async_copy(src, dst, local_sems.at[k])
        for k, (src, dst) in enumerate(
            (
                (attr_in, attr), (w1_in, w1), (hw_in, hw), (cb_in, cb), (w2_in, w2), (w3_in, w3),
                (cells_in, cells), (precip_in, precip), (temp_in, temp), (pet_in, pet),
            )
        )
    ]
    for copy in locals_:
        copy.start()
    got_attr, got_w1, got_hw, got_cb, got_w2, got_w3 = locals_[:6]

    edge = jnp.where(chan == 0, 0, NT - 1)
    far = NT - 1 - edge
    step = 1 - 2 * chan
    lacks = tile == edge
    gives = tile != far
    towards = jnp.where(gives, tile + step, tile - step)
    source = jnp.where(lacks, tile + step, tile - step)
    signal(barrier, chan=1 - chan)
    coords = [lax.rem(tile // weight, 4) for weight in LINES]
    earlier = coords[0] + coords[1] + coords[2]
    late_half = coords[2] // 2

    @pl.when(jnp.logical_not(lacks))
    def _():
        signal(barrier, tile=source)

    signal_line(barrier, tile, LINES, 1)

    place = lax.broadcasted_iota(jnp.int32, (W, W), 0)
    column = lax.broadcasted_iota(jnp.int32, (W, W), 1)
    perm[...] = ((place % SUB) * STEP + place // SUB == column).astype(F32).astype(BF16)
    wide1[...] = jnp.zeros(wide1.shape, BF16)
    wideh[...] = jnp.zeros(wideh.shape, BF16)
    for g in range(4):
        spread[g, A * GAP :, :] = jnp.zeros((48 * GAP - A * GAP, 128), F32)
    for wide in (wide2, wide3):
        wide[0:128, 1152:1536] = jnp.zeros((128, 384), BF16)
        wide[128:256, 0:384] = jnp.zeros((128, 384), BF16)

    def place_rows(first, last):
        for i in range(first, last):
            r = jnp.where(chan == 0, i, TH - 1 - i)
            for g in range(4):
                part = spread[g, pl.ds(r, 48, stride=GAP), :]
                slots[(3 + i) * CP : (3 + i) * CP + 48, g * 128 : (g + 1) * 128] = part.astype(BF16)
            slots[(3 + i) * CP + 48 : (4 + i) * CP, :] = jnp.zeros((CP - 48, W), BF16)

    got_attr.wait()
    for c in range(A):
        field = attr[c].astype(F32)
        for g in range(4):
            spread[g, c * GAP : c * GAP + TH, :] = field[:, g * 128 : (g + 1) * 128]
    place_rows(13, 16)

    pl.semaphore_wait(barrier, 1 + earlier + gives.astype(jnp.int32))
    weights = [
        pltpu.make_async_remote_copy(
            src_ref=src,
            dst_ref=dst,
            send_sem=w_send.at[k],
            recv_sem=w_recv.at[k],
            device_id={"chan": 1 - chan},
            device_id_type=MESH,
        )
        for k, (src, dst) in enumerate(((w1_in, w1r), (hw_in, hwr), (w2_in, w2r), (w3_in, w3r)))
    ]
    for copy in weights:
        copy.start()
    halos = [
        pltpu.make_async_remote_copy(
            src_ref=slots.at[pl.ds((16 + k) * CP, 48)],
            dst_ref=slots.at[pl.ds(k * CP, 48)],
            send_sem=halo_send.at[k],
            recv_sem=halo_recv.at[k],
            device_id={"tile": towards},
            device_id_type=MESH,
        )
        for k in range(3)
    ]

    @pl.when(gives)
    def _():
        for copy in halos:
            copy.start()

    signal_line(line_sem, tile, LINES, -1)
    for k in range(3):
        slots[k * CP + 48 : (k + 1) * CP, :] = jnp.zeros((CP - 48, W), BF16)

    @pl.when(lacks)
    def _():
        for k in range(3):
            slots[k * CP : k * CP + 48, :] = jnp.zeros((48, W), BF16)

    place_rows(0, 11)

    def arrange(block, count):
        at = 2 * block * CP
        a = dot_nt(perm[...], slots[at : at + count * 2 * CP, :])
        for k in range(count):
            put_row(h0, block + k, a[:, k * 128 : (k + 1) * 128])

    arrange(2, 2)
    arrange(4, 2)
    arrange(6, 1)


    @pl.when(earlier < 9)
    def _():
        pl.semaphore_wait(line_sem, 9 - earlier)

    for k in range(1, 4):
        signal(z_sem, tile=tile + (lax.rem(coords[1] + k, 4) - coords[1]) * 4)

    sub8 = lax.broadcasted_iota(jnp.int32, (HALF, 128), 0)
    lane8 = lax.broadcasted_iota(jnp.int32, (HALF, 128), 1)
    mine8 = lane8 // 16 == jnp.where(chan == 0, sub8, HALF - 1 - sub8)
    sub16 = lax.broadcasted_iota(jnp.int32, (SUB, 128), 0)
    got_cb.wait()
    own = cb[pl.ds(pl.multiple_of(chan * HALF, HALF), HALF), :]
    ids1, ids2, owners = [], [], []
    limit = jnp.zeros((SUB, 128), F32)
    for g in range(4):
        run = own[:, g * 128 : (g + 1) * 128]
        first = run[:, :1]
        last = run[:, 127:]
        count = jnp.sum((run == first).astype(F32), axis=1, keepdims=True)
        count = jnp.where(mine8, jnp.broadcast_to(count, (HALF, 128)), 0.0)
        count = jnp.sum(count, axis=0, keepdims=True)
        limit = jnp.where(sub16 // 4 == g, jnp.broadcast_to(count, (SUB, 128)), limit)
        owners.append(first // 128)
        ids1.append((first % 128).astype(F32))
        ids2.append((last % 128).astype(F32))
    limit = limit - ((sub16 % 4) * STEP).astype(F32)

    def widen(mine, theirs, wide):
        for half, ref in ((chan, mine), (1 - chan, theirs)):
            for t in range(9):
                dy, dx = t // 3, t % 3
                w = ref[jnp.where(chan == 0, dy, 2 - dy), dx]
                for e in range(2):
                    at = ((dy + e) * 3 + dx) * 128
                    wide[pl.ds(pl.multiple_of(e * 128 + half * 64, 64), 64), at : at + 128] = w

    def both(mine, theirs):
        left = jnp.where(chan == 0, mine, theirs)
        right = jnp.where(chan == 0, theirs, mine)
        return jnp.concatenate([left, right], axis=1)

    for copy in (got_w1, got_w2, got_w3, got_hw):
        copy.wait()
    for copy in weights:
        copy.wait_recv()
    for t in range(9):
        dy, dx = t // 3, t % 3
        at = jnp.where(chan == 0, dy, 2 - dy)
        w = both(w1[at, dx].astype(F32), w1r[at, dx].astype(F32)).astype(BF16)
        for e in range(2):
            row = dy + e
            at = ((row // 2) * 3 + dx) * 128 + (row % 2) * CP
            wide1[at : at + A, e * 128 : (e + 1) * 128] = w
    widen(w2, w2r, wide2)
    widen(w3, w3r, wide3)
    w = both(hw[...].astype(F32), hwr[...].astype(F32)).astype(BF16)
    for r in range(HALF):
        wideh[r * 16 : r * 16 + 12, r * 128 : (r + 1) * 128] = w

    def taps(src, pair):
        return jnp.concatenate(
            [
                src[2 * pair + dy, dx * SUB : dx * SUB + W, :]
                for dy in range(4)
                for dx in range(3)
            ],
            axis=1,
        )

    def conv1(pair, keep=None):
        lhs = jnp.concatenate(
            [h0[pair + b, dx * SUB : dx * SUB + W, :] for b in range(2) for dx in range(3)], axis=1
        )
        put_pair(h1, pair, jnp.maximum(dot(lhs, wide1[...]), 0.0), keep)

    def conv2(pair, keep=None):
        put_pair(h2, pair, jnp.maximum(dot_nt(taps(h1, pair), wide2[...]), 0.0), keep)

    def conv3(pair):
        h3[pair] = jnp.maximum(dot_nt(taps(h2, pair), wide3[...]), 0.0).astype(BF16)

    for pair in range(2, 6):
        conv1(pair)
    for pair in range(2, 5):
        conv2(pair)
    pl.semaphore_wait(z_sem, 3)
    for k in range(1, 4):
        peer = tile + (lax.rem(coords[2] + k, 4) - coords[2]) * 16
        signal(y_sem.at[late_half], tile=peer)
        signal(y_sem.at[late_half], tile=peer, chan=1 - chan)
    signal(y_sem.at[late_half], chan=1 - chan)
    for pair in range(2, 4):
        conv3(pair)

    @pl.when(jnp.logical_not(lacks))
    def _():
        for copy in halos:
            copy.wait_recv()

    arrange(0, 2)
    inside = 1.0 - lacks.astype(F32)
    conv1(1)
    conv1(0, (inside, inside))
    conv2(1)
    conv2(0, (inside, 1.0))
    conv3(1)
    conv3(0)

    share = jax.nn.sigmoid(
        dot_nt(jnp.concatenate([h3[q] for q in range(4)], axis=1), wideh[...])
    )
    sums = [jnp.zeros((SUB, 128), F32), jnp.zeros((SUB, 128), F32)]
    for j in range(STEP):
        v = share[j * SUB : (j + 1) * SUB]
        inside = limit > j
        sums[0] = sums[0] + jnp.where(inside, v, 0.0)
        sums[1] = sums[1] + jnp.where(inside, 0.0, v)
    rows = []
    for g in range(4):
        pair = []
        for s, ids in zip(sums, (ids1, ids2)):
            v = jnp.sum(s[4 * g : 4 * g + 4], axis=0, keepdims=True)
            v = jnp.where(mine8, jnp.broadcast_to(v, (HALF, 128)), 0.0)
            for shift in (64, 32, 16):
                v = v + pltpu.roll(v, shift, axis=1)
            pair.append(jnp.where(lane8 % 16 == 12, jnp.broadcast_to(ids[g], (HALF, 128)), v))
        rows.append(jnp.where((lane8 // 16) % 2 == 0, pair[0], pair[1]))
    value = jnp.concatenate(rows, axis=0)
    hi = value.astype(BF16).astype(F32)
    mid = (value - hi).astype(BF16).astype(F32)
    low = value - hi - mid
    kind = lax.broadcasted_iota(jnp.int32, (32, 128), 1) // 32
    parts = jnp.where(kind == 0, hi, jnp.where(kind == 1, mid, jnp.where(kind == 2, low, 0.0)))
    to_owner = jnp.concatenate(
        [(jnp.broadcast_to(o, (HALF, 128)) == lane8).astype(F32) for o in owners], axis=0
    )
    routed = dot_tn(to_owner.astype(BF16), parts.astype(BF16))[:NT]
    sendb[...] = routed.reshape(NT, 1, 128)

    me = chan * NT + tile
    recvb[me] = sendb[tile]
    mine_at = greet_order(tile) * 2 + chan

    def send_row(o, c):
        pltpu.make_async_remote_copy(
            src_ref=sendb.at[o],
            dst_ref=recvb.at[me],
            send_sem=row_send,
            recv_sem=row_recv,
            device_id={"tile": o, "chan": c},
            device_id_type=MESH,
        ).start()

    for half in range(2):
        pl.semaphore_wait(y_sem.at[half], jnp.where(late_half == half, 3, 4))
        last = (half + 1) * NT - 1
        for i in range(half * NT, last):
            swap = mine_at == i
            o = jnp.where(swap, greet_tile(last // 2), greet_tile(i // 2))
            send_row(o, jnp.where(swap, last % 2, i % 2))

        @pl.when(late_half != half)
        def _():
            send_row(greet_tile(last // 2), last % 2)

    rest = pl.ds(0, 2 * NT - 1)
    pltpu.make_async_copy(recvb.at[rest], recvb.at[rest], row_recv).wait()
    got = recvb[...].reshape(2, NT, 128)
    got = got[0] + got[1]
    basin = lax.broadcasted_iota(jnp.int32, (NT, 128), 1).astype(F32)
    gotb = got.astype(BF16)
    total = jnp.zeros((16, 128), F32)
    for b in range(2):
        hit = (jnp.broadcast_to(got[:, 16 * b + 12 : 16 * b + 13], (NT, 128)) == basin).astype(F32)
        placed = dot_tn(gotb, hit.astype(BF16))
        for k in range(3):
            total = total + placed[32 * k + 16 * b : 32 * k + 16 * b + 16]

    for copy in locals_[6:]:
        copy.wait()
    bucket(total, cells[...], precip, temp, pet, out)

    pltpu.make_async_copy(recvb.at[rest], recvb.at[rest], row_send).wait()

    @pl.when(gives)
    def _():
        for copy in halos:
            copy.wait_send()

    for copy in weights:
        copy.wait_send()


def bucket(sums, cells, precip, temp, pet, out):
    mean = sums / cells.astype(F32)
    shape = (8, 128)
    param = [LOW[p] + SPAN[p] * mean[p : p + 1] for p in range(12)]
    tt, cfmax, fc, beta, lp, k0, k1, k2, uzl, perc = [
        jnp.broadcast_to(param[p], shape) for p in range(10)
    ]
    raw = [
        jnp.exp((param[10] - 1.0) * jnp.log(jnp.float32(k + 0.5)) - (k + 0.5) / param[11])
        for k in range(LAGS)
    ]
    total = raw[0]
    for k in range(1, LAGS):
        total = total + raw[k]
    kernel = [jnp.broadcast_to(r / total, shape) for r in raw]
    dry = lp * fc
    per_dry = 1.0 / dry
    per_fc = 1.0 / fc
    power = beta * 1.4426950408889634
    snow = jnp.zeros(shape, F32)
    soil = jnp.full(shape, 0.5, F32)
    upper = jnp.full(shape, 5.0, F32)
    lower = jnp.full(shape, 20.0, F32)
    runoff = []
    for d in range(precip.shape[0]):
        rain, air, demand = precip[d], temp[d], pet[d]
        warm = air - tt
        liquid = jax.nn.sigmoid(warm)
        wet = rain * liquid
        gained = snow + (rain - wet)
        snow = jnp.maximum(gained - cfmax * jnp.maximum(warm, 0.0), 0.0)
        inflow = wet + (gained - snow)
        share = jnp.exp2(power * jnp.log(soil))
        recharge = inflow * share
        filled = soil + inflow * per_fc
        filled = filled - (inflow * per_fc) * share
        excess = jnp.maximum(filled - 1.0, 0.0) * fc
        soil = jnp.minimum(filled, 1.0)
        soil = jnp.where(soil < lp, soil * (1.0 - demand * per_dry), soil - demand * per_fc)
        upper = upper + recharge + excess
        upper_new = jnp.maximum(upper - perc, 0.0)
        lower = lower + upper - upper_new
        quick = k0 * jnp.maximum(upper_new - uzl, 0.0)
        slow = k1 * upper_new
        upper = upper_new - quick - slow
        base = k2 * lower
        lower = lower - base
        runoff.append(quick + slow + base)
        flow = kernel[0] * runoff[d]
        for k in range(1, min(d, LAGS - 1) + 1):
            flow = flow + kernel[k] * runoff[d - k]
        out[d] = flow


def on_device(
    attributes, cell_basin, basin_cells, conv_first, conv_second, conv_third, head_weight,
    precip, temp, pet,
):
    args = (
        attributes,
        cell_basin,
        basin_cells.reshape(1, 128),
        jnp.transpose(conv_first, (1, 2, 3, 0)),
        jnp.transpose(conv_second, (1, 2, 0, 3)),
        jnp.transpose(conv_third, (1, 2, 0, 3)),
        head_weight.T,
        precip,
        temp,
        pet,
    )
    held = [pltpu.VMEM(a.shape, a.dtype) for a in args]
    theirs = [pltpu.VMEM(args[k].shape, BF16) for k in (3, 4, 5, 6)]
    return pl.pallas_call(
        raster_kernel,
        out_shape=pltpu.VMEM(precip.shape, F32),
        in_specs=[pl.BlockSpec(memory_space=pltpu.HBM)] * len(args),
        out_specs=pl.BlockSpec(memory_space=pltpu.VMEM),
        scratch_shapes=held
        + theirs
        + [
            pltpu.VMEM((4, 48 * GAP, 128), F32),
            pltpu.VMEM((19 * CP, W), BF16),
            pltpu.VMEM((W, W), BF16),
            pltpu.VMEM((768, 256), BF16),
            pltpu.VMEM((256, 1536), BF16),
            pltpu.VMEM((256, 1536), BF16),
            pltpu.VMEM((128, 1024), BF16),
            pltpu.VMEM((7, WP, 128), BF16),
            pltpu.VMEM((12, WP, 128), BF16),
            pltpu.VMEM((10, WP, 128), BF16),
            pltpu.VMEM((4, W, 256), BF16),
            pltpu.VMEM((NT, 1, 128), F32),
            pltpu.VMEM((2 * NT, 1, 128), F32),
            pltpu.SemaphoreType.DMA((10,)),
            pltpu.SemaphoreType.DMA((3,)),
            pltpu.SemaphoreType.DMA((3,)),
            pltpu.SemaphoreType.DMA((4,)),
            pltpu.SemaphoreType.DMA((4,)),
            pltpu.SemaphoreType.DMA,
            pltpu.SemaphoreType.DMA,
            pltpu.SemaphoreType.REGULAR,
            pltpu.SemaphoreType.REGULAR,
            pltpu.SemaphoreType.REGULAR((2,)),
        ],
        compiler_params=pltpu.CompilerParams(
            collective_id=0, has_side_effects=True, vmem_limit_bytes=56 * 1024 * 1024
        ),
        name="raster",
    )(*args)


def solution(mesh):
    return jax.shard_map(
        on_device,
        mesh=mesh,
        in_specs=(
            P(None, "tile", None),
            P("tile", None),
            P("tile"),
            P("chan", None, None, None),
            P("chan", None, None, None),
            P("chan", None, None, None),
            P("chan", None),
            P(None, "chan", "tile"),
            P(None, "chan", "tile"),
            P(None, "chan", "tile"),
        ),
        out_specs=P(None, "chan", "tile"),
        check_vma=False,
    )
```
